512 devices in a mesh: cell: 64 (over z, y_lo, core), inst: 8 (over x, y_hi).
Axes of the slice: x: 4, y: 4 (y_hi: 2, y_lo: 2; y = y_hi * 2 + y_lo), z: 16, core: 2. Of those that a mesh axis runs over, the one named last changes fastest.
Arguments:
- initial: float32 [80, 131072], P('inst', 'cell'), may hold values from -6 to 6
- source: float32 [80, 131072], P('inst', 'cell'), may hold values from -6 to 6
- neighbors: int32 [4, 131072], P(None, 'cell'), may hold values from -256 to 256, as said below
- face_weights: float32 [4, 131072], P(None, 'cell'), may hold values from 0.25 to 1
- damping: float32 [131072], P('cell'), may hold values from 0.5 to 2
Outputs:
- solution: float32 [80, 131072], P('inst', 'cell')
The draws below stay inside these ranges and needn't reach their ends.
Inputs may be any that keep to these rules, and one draw needn't show every extreme that they name: `neighbors`: entries 0 and 2 of a cell's offsets are at or below zero, entries 1 and 3 at or above zero; a cell plus each of its offsets is a cell of the grid; in every draw some offsets are exactly -256 and exactly 256.
All inputs are finite; a program needn't handle non-finite values.
Results may differ from the reference program's by a relative error of at most 0.0001.
Values sent between devices are 32-bit elements; how exact they have to be, the bound alone decides.
A program may use at most 64 MiB of HBM per device.

```python
import math
import jax
import jax.numpy as jnp
from jax import lax

NI = 16
NC = 4
COMP = 5
NEIGH = 4
SWEEPS_FINE = 2
SWEEPS_COARSE = 3
PLANE = 256
NCELLS = 131072


def draw_neighbors(key, part):
    number = jnp.arange(NCELLS, dtype=jnp.int32)
    key_near, key_far = jax.random.split(jax.random.fold_in(key, 17))
    near = jax.random.randint(key_near, (2, NCELLS), 1, 9, dtype=jnp.int32)
    far = PLANE - jax.random.randint(key_far, (2, NCELLS), 0, max(PLANE // 2, 1), dtype=jnp.int32)
    far = jnp.where((number % 4 == 0)[None, :], PLANE, far)
    offsets = jnp.stack([-near[0], near[1], -far[0], far[1]])
    target = jnp.clip(number[None, :] + offsets, 0, NCELLS - 1)
    return (target - number[None, :]).astype(jnp.int32)


def level_of(key, dims, shards, smallest, top_value):
    loudness, own = 1.0, jax.random.fold_in(key, 6)
    for dim, parts in shards:
        steps = jnp.exp(jax.random.uniform(jax.random.fold_in(own, dim), (parts,), jnp.float32, smallest / len(shards), top_value / len(shards)))
        loudness = loudness * jnp.repeat(steps, dims[dim] // parts).reshape([-1 if axis == dim else 1 for axis in range(len(dims))])
    return loudness


def noise(stream_key, shape, scale, most, cuts=(), kind=jnp.bfloat16):
    level = level_of(stream_key, shape, cuts, -0.22, 0.18) if cuts else 1.0
    entries = jax.random.normal(stream_key, shape, jnp.float32) * scale * level
    return jnp.minimum(jnp.maximum(entries, -most), most).astype(kind)


def setup_inputs(seed: int = 0) -> dict:
    splits = jax.random.split(jax.random.key(seed), 6)
    return {
        "initial": noise(splits[0], (NI * COMP, NCELLS), 1.0, 6.0, ((0, 8), (1, 64)), jnp.float32),
        "source": noise(splits[1], (NI * COMP, NCELLS), 1.0, 6.0, ((0, 8), (1, 64)), jnp.float32),
        "neighbors": draw_neighbors(jax.random.fold_in(splits[5], 71), 0),
        "face_weights": jnp.clip(jnp.exp(math.log(1.0) - 1.3862944 * jax.random.uniform(splits[3], (NEIGH, NCELLS), jnp.float32) ** level_of(splits[3], (NEIGH, NCELLS), ((1, 64),), -0.2, 0.2)), 0.25, 1.0),
        "damping": jnp.clip(jnp.exp(math.log(2.0) - 1.3862944 * jax.random.uniform(splits[4], (NCELLS,), jnp.float32) ** level_of(splits[4], (NCELLS,), ((0, 64),), -0.2, 0.2)), 0.5, 2.0),
    }


FREQ = 0.15
RELAX = 0.6


def spectral_matrix(points):
    steps = jnp.arange(points, dtype=jnp.float32)
    offset = steps[:, None] - steps[None, :]
    parity = 1.0 - 2.0 * jnp.mod(offset, 2.0)
    angle = jnp.where(offset == 0, 0.5, jnp.pi * offset / points)
    return jnp.where(offset == 0, 0.0, 0.5 * parity / jnp.tan(angle))


def restrict_matrix():
    coarse_t = jnp.arange(NC, dtype=jnp.float32) / NC
    fine_t = jnp.arange(NI, dtype=jnp.float32) / NI
    return (1.0 + 2.0 * jnp.cos(2.0 * jnp.pi * (coarse_t[:, None] - fine_t[None, :]))) / NI


def prolong_matrix():
    coarse_t = jnp.arange(NC, dtype=jnp.float32) / NC
    fine_t = jnp.arange(NI, dtype=jnp.float32) / NI
    return (1.0 + 2.0 * jnp.cos(2.0 * jnp.pi * (fine_t[:, None] - coarse_t[None, :]))) / NC


def neighbour_terms(values, neighbors, face_weights):
    number = jnp.arange(values.shape[1], dtype=jnp.int32)
    summed = jnp.zeros(values.shape, jnp.float32)
    for slot in range(NEIGH):
        target = (number + neighbors[slot].astype(jnp.int32)).astype(jnp.int32)
        summed = summed + face_weights[slot] * jnp.take(values, target, axis=1)
    return summed


def operate(values, matrix, neighbors, face_weights, diagonal):
    points = matrix.shape[0]
    shaped = values.reshape(points, COMP, values.shape[1])
    spectral = jnp.einsum("nm,mcx->ncx", matrix, shaped, precision=lax.Precision.HIGHEST).reshape(values.shape)
    return FREQ * spectral + diagonal * values - neighbour_terms(values, neighbors, face_weights)


def reference(initial, source, neighbors, face_weights, damping):
    cells = initial.shape[1]
    diagonal = damping + jnp.sum(face_weights, axis=0)
    fine_matrix = spectral_matrix(NI)
    coarse_matrix = spectral_matrix(NC)
    solution = initial
    for sweep in range(SWEEPS_FINE):
        solution = solution + RELAX * (source - operate(solution, fine_matrix, neighbors, face_weights, diagonal)) / diagonal
    residual = source - operate(solution, fine_matrix, neighbors, face_weights, diagonal)
    coarse_rhs = jnp.einsum("jm,mcx->jcx", restrict_matrix(), residual.reshape(NI, COMP, cells), precision=lax.Precision.HIGHEST).reshape(NC * COMP, cells)
    correction = RELAX * coarse_rhs / diagonal
    for sweep in range(SWEEPS_COARSE - 1):
        correction = correction + RELAX * (coarse_rhs - operate(correction, coarse_matrix, neighbors, face_weights, diagonal)) / diagonal
    lifted = jnp.einsum("mj,jcx->mcx", prolong_matrix(), correction.reshape(NC, COMP, cells), precision=lax.Precision.HIGHEST)
    return solution + lifted.reshape(NI * COMP, cells)
```

```python
import math

import jax
import jax.numpy as jnp
from jax import lax
from jax.experimental import pallas as pl
from jax.experimental.pallas import tpu as pltpu
from jax.sharding import PartitionSpec as P

NI = 16
COMP = 5
NEIGH = 4
FREQ = 0.15
RELAX = 0.6
LANES = 128
OWN = 16
RIM = 4
WIDE = 8
ROWS = OWN + 2 * WIDE
GROUP = 8
PER = NI // GROUP
LOW = 3
MESH = pl.DeviceIdType.MESH
ROOT = math.sqrt(0.5)


def forward(x):
    out = [None] * NI
    p = [x[n] + x[n + 8] for n in range(8)]
    q = [x[n] - x[n + 8] for n in range(8)]
    q0, q4 = q[0] * 0.125, q[4] * 0.125
    d = [None] + [q[n] - q[8 - n] for n in (1, 2, 3)]
    s = [None] + [q[n] + q[8 - n] for n in (1, 2, 3)]
    for k in (1, 3, 5, 7):
        a, b = q0, (q4 if k in (1, 5) else -q4)
        for n in (1, 2, 3):
            a = a + d[n] * (math.cos(math.pi * k * n / 8) / 8)
            b = b + s[n] * (math.sin(math.pi * k * n / 8) / 8)
        out[2 * k - 1], out[2 * k] = a, b
    pp = [p[n] + p[n + 4] for n in range(4)]
    pq = [p[n] - p[n + 4] for n in range(4)]
    a, b = pq[0] * 0.125, pq[2] * 0.125
    d1, s1 = (pq[1] - pq[3]) * (ROOT / 8), (pq[1] + pq[3]) * (ROOT / 8)
    out[3], out[4] = a + d1, s1 + b
    out[11], out[12] = a - d1, s1 - b
    out[7], out[8] = (pp[0] - pp[2]) * 0.125, (pp[1] - pp[3]) * 0.125
    even, odd = (pp[0] + pp[2]) * 0.0625, (pp[1] + pp[3]) * 0.0625
    out[0], out[15] = even + odd, even - odd
    return out


def backward(h):
    a = {k: h[2 * k - 1] for k in range(1, 9)}
    a[0] = h[0]
    b = {k: h[2 * k] for k in range(1, 8)}
    odd = [None] * 8
    odd[0] = (a[1] + a[3]) + (a[5] + a[7])
    odd[4] = (b[1] - b[3]) + (b[5] - b[7])
    for n in (1, 2, 3):
        c = s = 0.0
        for k in (1, 3, 5, 7):
            c = c + a[k] * math.cos(math.pi * k * n / 8)
            s = s + b[k] * math.sin(math.pi * k * n / 8)
        odd[n], odd[8 - n] = s + c, s - c
    d, s = (a[2] - a[6]) * ROOT, (b[2] + b[6]) * ROOT
    half = [a[2] + a[6], s + d, b[2] - b[6], s - d]
    up, down = a[0] + a[8], a[0] - a[8]
    quarter = [up + a[4], down + b[4], up - a[4], down - b[4]]
    even = [quarter[n] + half[n] for n in range(4)] + [quarter[n] - half[n] for n in range(4)]
    return [even[n] + odd[n] for n in range(8)] + [even[n] - odd[n] for n in range(8)]


def owner(variable, cell):
    return variable + 3 * lax.rem(cell, 2)


def kernel(
    initial, source, neighbors, weights, damping, out,
    sx, sl, sr, stl, str_, ro, rl, rr, rstl, rstr,
    lane, step, gain, scale, u0, u1, src, low2, low3, low4, fin, back,
    s_own, s_left, s_right, s_stat, r_own, r_left, r_right, r_stat, s_low, r_low, s_out, r_out,
):
    cell, inst = lax.axis_index("cell"), lax.axis_index("inst")
    count = lax.axis_size("cell")
    after, before = lax.rem(cell + 1, count), lax.rem(cell + count - 1, count)
    mine = inst - 3 * lax.rem(cell, 2)
    busy = jnp.logical_and(mine >= 0, mine < COMP)

    def at(c, i):
        return {"cell": c, "inst": i}

    barrier = pltpu.get_barrier_semaphore()

    def greet(c, i):
        pl.semaphore_signal(barrier, inc=1, device_id=at(c, i), device_id_type=MESH)

    @pl.when(busy)
    def _():
        for j in range(1, GROUP):
            greet(cell, lax.rem(inst + j, GROUP))
        for c in (before, after):
            for i in range(GROUP):
                greet(c, i)

    @pl.when(jnp.logical_not(busy))
    def _():
        for v in range(COMP):
            greet(cell, owner(v, cell))

    for which, ref in enumerate((initial, source)):
        for n in range(PER):
            for v in range(COMP):
                x = ref[pl.ds(n * COMP + v, 1), :].reshape(OWN, LANES)
                sx[v, which, n] = x
                sl[v, which, n] = x[OWN - RIM :]
                sr[v, which, n] = x[:RIM]

    w = [weights[pl.ds(k, 1), :].reshape(OWN, LANES) for k in range(NEIGH)]
    off = [neighbors[pl.ds(k, 1), :].reshape(OWN, LANES) for k in range(NEIGH)]
    m = RELAX / (damping[...] + ((w[0] + w[1]) + (w[2] + w[3])))
    scale[WIDE : WIDE + OWN] = m
    stl[2 * NEIGH], str_[2 * NEIGH] = m[OWN - RIM :], m[:RIM]
    for k in range(NEIGH):
        g = w[k] * m
        position = lax.broadcasted_iota(jnp.int32, (OWN, LANES), 1) + off[k]
        lane[k, WIDE : WIDE + OWN] = position & (LANES - 1)
        step[k, WIDE : WIDE + OWN] = position >> 7
        gain[k, WIDE : WIDE + OWN] = g
        f = off[k].astype(jnp.float32)
        stl[k], str_[k] = f[OWN - RIM :], f[:RIM]
        stl[NEIGH + k], str_[NEIGH + k] = g[OWN - RIM :], g[:RIM]

    @pl.when(busy)
    def _():
        pl.semaphore_wait(barrier, 17)

    @pl.when(jnp.logical_not(busy))
    def _():
        pl.semaphore_wait(barrier, 15)

    def remote(a, b, s, r, c, i):
        return pltpu.make_async_remote_copy(
            src_ref=a, dst_ref=b, send_sem=s, recv_sem=r, device_id=at(c, i), device_id_type=MESH
        )

    own_copy = [
        remote(sx.at[v], ro.at[inst], s_own.at[v], r_own.at[inst], cell, owner(v, cell)) for v in range(COMP)
    ]
    left_copy = [
        remote(sl.at[v], rl.at[inst], s_left.at[v], r_left.at[inst], after, owner(v, after)) for v in range(COMP)
    ]
    right_copy = [
        remote(sr.at[v], rr.at[inst], s_right.at[v], r_right.at[inst], before, owner(v, before)) for v in range(COMP)
    ]
    for v in range(COMP):
        left_copy[v].start()
        right_copy[v].start()

        @pl.when(mine != v)
        def _():
            own_copy[v].start()

    @pl.when(busy)
    def _():
        stat = [
            remote(stl, rstl, s_stat.at[0], r_stat.at[0], after, owner(mine, after)),
            remote(str_, rstr, s_stat.at[1], r_stat.at[1], before, owner(mine, before)),
        ]
        keep = pltpu.make_async_copy(sx.at[mine], ro.at[inst], r_own.at[inst])
        keep.start()
        for copy in stat:
            copy.start()
        for copy in stat:
            copy.wait_recv()
        for start, got in ((WIDE - RIM, rstl), (WIDE + OWN, rstr)):
            rows = pl.ds(start, RIM)
            for k in range(NEIGH):
                position = lax.broadcasted_iota(jnp.int32, (RIM, LANES), 1) + got[k].astype(jnp.int32)
                lane[k, rows] = position & (LANES - 1)
                step[k, rows] = position >> 7
                gain[k, rows] = got[NEIGH + k]
            scale[rows] = got[2 * NEIGH]

        def arrived(ref, sem):
            for j in range(GROUP):
                pltpu.make_async_copy(ref.at[j], ref.at[j], sem.at[j]).wait()

        def transform(ref, first, rows, to):
            for which, dst in ((0, u0), (1, src)):
                h = forward([ref[n // PER, which, n % PER, pl.ds(first, rows)] for n in range(NI)])
                for j in range(NI):
                    dst[j, pl.ds(to, rows)] = h[j]

        arrived(rl, r_left)
        transform(rl, 0, RIM, WIDE - RIM)
        arrived(rr, r_right)
        transform(rr, 0, RIM, WIDE + OWN)
        arrived(ro, r_own)
        for t in range(OWN // 8):
            transform(ro, 8 * t, 8, WIDE + 8 * t)

        def sweep(old, new, start, to, harmonics):
            rows = pl.ds(start, 8)
            lanes = [lane[k, rows] for k in range(NEIGH)]
            steps = [step[k, rows] for k in range(NEIGH)]
            near = [steps[k] == 0 for k in range(NEIGH)]
            next_ = [steps[k] == (1 if k % 2 else -1) for k in range(NEIGH)]
            gains = [gain[k, rows] for k in range(NEIGH)]
            m = scale[rows]

            def coupled(j):
                x = {d: old[j, pl.ds(start + d, 8)] for d in (-2, -1, 0, 1, 2)}
                total = x[0] * (1.0 - RELAX)
                for k in range(NEIGH):
                    sign = 1 if k % 2 else -1
                    pick = [jnp.take_along_axis(x[sign * d], lanes[k], axis=1, mode="promise_in_bounds") for d in range(3)]
                    total = total + gains[k] * jnp.where(near[k], pick[0], jnp.where(next_[k], pick[1], pick[2]))
                return x[0], total

            for k in harmonics:
                if k in (0, 8):
                    j = max(2 * k - 1, 0)
                    _, total = coupled(j)
                    new[j, pl.ds(to, 8)] = total + m * src[j, rows]
                else:
                    a, b = 2 * k - 1, 2 * k
                    xa, ta = coupled(a)
                    xb, tb = coupled(b)
                    new[a, pl.ds(to, 8)] = ta + m * (src[a, rows] - (FREQ * k) * xb)
                    new[b, pl.ds(to, 8)] = tb + m * (src[b, rows] + (FREQ * k) * xa)

        low, high = (0, 1), tuple(range(2, 9))
        for start in (6, 14, 18):
            sweep(u0, u1, start, start, low)
        for start in (8, 16):
            sweep(u1, low2, start, start, low)
        wide = [
            remote(low2.at[:, pl.ds(OWN, WIDE)], low2.at[:, pl.ds(0, WIDE)], s_low.at[0], r_low.at[0], after, owner(mine, after)),
            remote(low2.at[:, pl.ds(WIDE, WIDE)], low2.at[:, pl.ds(WIDE + OWN, WIDE)], s_low.at[1], r_low.at[1], before, owner(mine, before)),
        ]
        for copy in wide:
            copy.start()
        for start in (6, 14, 18):
            sweep(u0, u1, start, start, high)
        for start in (8, 16):
            sweep(u1, fin, start, start - WIDE, high)
        for copy in wide:
            copy.wait_recv()
        for start in (4, 12, 20):
            sweep(low2, low3, start, start, low)
        for start in (6, 14, 18):
            sweep(low3, low4, start, start, low)
        for start in (8, 16):
            sweep(low4, fin, start, start - WIDE, low)
        for t in range(OWN // 8):
            rows = pl.ds(8 * t, 8)
            x = backward([fin[j, rows] for j in range(NI)])
            for n in range(NI):
                back[n // PER, n % PER, rows] = x[n]
        home = [
            remote(back.at[i], out.at[:, mine], s_out.at[i], r_out.at[mine], cell, i) for i in range(GROUP)
        ]
        for i in range(GROUP):

            @pl.when(inst != i)
            def _():
                home[i].start()

        stay = pltpu.make_async_copy(back.at[inst], out.at[:, mine], r_out.at[mine])
        stay.start()
        for i in range(GROUP):

            @pl.when(inst != i)
            def _():
                home[i].wait_send()

        for copy in wide + stat:
            copy.wait_send()

    for v in range(COMP):
        left_copy[v].wait_send()
        right_copy[v].wait_send()

        @pl.when(mine != v)
        def _():
            own_copy[v].wait_send()

    for v in range(COMP):
        pltpu.make_async_copy(out.at[:, v], out.at[:, v], r_out.at[v]).wait()


def per_device(initial, source, neighbors, face_weights, damping):
    vmem = pl.BlockSpec(memory_space=pltpu.VMEM)
    f32, i32 = jnp.float32, jnp.int32
    dma = pltpu.SemaphoreType.DMA
    tall = (NI, ROWS, LANES)
    low = (LOW, ROWS, LANES)
    result = pl.pallas_call(
        kernel,
        out_shape=jax.ShapeDtypeStruct((PER, COMP, OWN, LANES), f32),
        in_specs=[vmem] * 5,
        out_specs=vmem,
        scratch_shapes=[
            pltpu.VMEM((COMP, 2, PER, OWN, LANES), f32),
            pltpu.VMEM((COMP, 2, PER, RIM, LANES), f32),
            pltpu.VMEM((COMP, 2, PER, RIM, LANES), f32),
            pltpu.VMEM((2 * NEIGH + 1, RIM, LANES), f32),
            pltpu.VMEM((2 * NEIGH + 1, RIM, LANES), f32),
            pltpu.VMEM((GROUP, 2, PER, OWN, LANES), f32),
            pltpu.VMEM((GROUP, 2, PER, RIM, LANES), f32),
            pltpu.VMEM((GROUP, 2, PER, RIM, LANES), f32),
            pltpu.VMEM((2 * NEIGH + 1, RIM, LANES), f32),
            pltpu.VMEM((2 * NEIGH + 1, RIM, LANES), f32),
            pltpu.VMEM((NEIGH, ROWS, LANES), i32),
            pltpu.VMEM((NEIGH, ROWS, LANES), i32),
            pltpu.VMEM((NEIGH, ROWS, LANES), f32),
            pltpu.VMEM((ROWS, LANES), f32),
            pltpu.VMEM(tall, f32),
            pltpu.VMEM(tall, f32),
            pltpu.VMEM(tall, f32),
            pltpu.VMEM(low, f32),
            pltpu.VMEM(low, f32),
            pltpu.VMEM(low, f32),
            pltpu.VMEM((NI, OWN, LANES), f32),
            pltpu.VMEM((GROUP, PER, OWN, LANES), f32),
            dma((COMP,)), dma((COMP,)), dma((COMP,)), dma((2,)),
            dma((GROUP,)), dma((GROUP,)), dma((GROUP,)), dma((2,)),
            dma((2,)), dma((2,)), dma((GROUP,)), dma((COMP,)),
        ],
        compiler_params=pltpu.CompilerParams(
            collective_id=0, has_side_effects=True, vmem_limit_bytes=32 * 1024 * 1024
        ),
    )(initial, source, neighbors, face_weights, damping.reshape(OWN, LANES))
    return result.reshape(PER * COMP, OWN * LANES)


def solution(mesh):
    return jax.shard_map(
        per_device,
        mesh=mesh,
        in_specs=(
            P("inst", "cell"),
            P("inst", "cell"),
            P(None, "cell"),
            P(None, "cell"),
            P("cell"),
        ),
        out_specs=P("inst", "cell"),
        check_vma=False,
    )
```

```python
import math

import jax
import jax.numpy as jnp
from jax import lax
from jax.experimental import pallas as pl
from jax.experimental.pallas import tpu as pltpu
from jax.sharding import PartitionSpec as P

NI = 16
COMP = 5
NEIGH = 4
FREQ = 0.15
RELAX = 0.6
LANES = 128
OWN = 16
RIM = 4
WIDE = 8
ROWS = OWN + 2 * WIDE
GROUP = 8
PER = NI // GROUP
LOW = 3
MESH = pl.DeviceIdType.MESH
ROOT = math.sqrt(0.5)


def forward(x):
    out = [None] * NI
    p = [x[n] + x[n + 8] for n in range(8)]
    q = [x[n] - x[n + 8] for n in range(8)]
    q0, q4 = q[0] * 0.125, q[4] * 0.125
    d = [None] + [q[n] - q[8 - n] for n in (1, 2, 3)]
    s = [None] + [q[n] + q[8 - n] for n in (1, 2, 3)]
    for k in (1, 3, 5, 7):
        a, b = q0, (q4 if k in (1, 5) else -q4)
        for n in (1, 2, 3):
            a = a + d[n] * (math.cos(math.pi * k * n / 8) / 8)
            b = b + s[n] * (math.sin(math.pi * k * n / 8) / 8)
        out[2 * k - 1], out[2 * k] = a, b
    pp = [p[n] + p[n + 4] for n in range(4)]
    pq = [p[n] - p[n + 4] for n in range(4)]
    a, b = pq[0] * 0.125, pq[2] * 0.125
    d1, s1 = (pq[1] - pq[3]) * (ROOT / 8), (pq[1] + pq[3]) * (ROOT / 8)
    out[3], out[4] = a + d1, s1 + b
    out[11], out[12] = a - d1, s1 - b
    out[7], out[8] = (pp[0] - pp[2]) * 0.125, (pp[1] - pp[3]) * 0.125
    even, odd = (pp[0] + pp[2]) * 0.0625, (pp[1] + pp[3]) * 0.0625
    out[0], out[15] = even + odd, even - odd
    return out


def backward(h):
    a = {k: h[2 * k - 1] for k in range(1, 9)}
    a[0] = h[0]
    b = {k: h[2 * k] for k in range(1, 8)}
    odd = [None] * 8
    odd[0] = (a[1] + a[3]) + (a[5] + a[7])
    odd[4] = (b[1] - b[3]) + (b[5] - b[7])
    for n in (1, 2, 3):
        c = s = 0.0
        for k in (1, 3, 5, 7):
            c = c + a[k] * math.cos(math.pi * k * n / 8)
            s = s + b[k] * math.sin(math.pi * k * n / 8)
        odd[n], odd[8 - n] = s + c, s - c
    d, s = (a[2] - a[6]) * ROOT, (b[2] + b[6]) * ROOT
    half = [a[2] + a[6], s + d, b[2] - b[6], s - d]
    up, down = a[0] + a[8], a[0] - a[8]
    quarter = [up + a[4], down + b[4], up - a[4], down - b[4]]
    even = [quarter[n] + half[n] for n in range(4)] + [quarter[n] - half[n] for n in range(4)]
    return [even[n] + odd[n] for n in range(8)] + [even[n] - odd[n] for n in range(8)]


def owner(variable, cell):
    return variable + 3 * lax.rem(cell, 2)


def kernel(
    initial_in, source_in, neighbors_in, weights_in, damping_in, out,
    initial, source, neighbors, weights, damping,
    sx, sl, sr, stl, str_, ro, rl, rr, rstl, rstr,
    lane, step, gain, scale, u0, u1, src, low2, low3, low4, fin, back,
    s_in, s_own, s_left, s_right, s_stat, r_own, r_left, r_right, r_stat, s_low, r_low, s_out, r_out,
):
    cell, inst = lax.axis_index("cell"), lax.axis_index("inst")
    count = lax.axis_size("cell")
    first, last = cell == 0, cell == count - 1
    has_before, has_after = jnp.logical_not(first), jnp.logical_not(last)
    after, before = jnp.minimum(cell + 1, count - 1), jnp.maximum(cell - 1, 0)
    sides = has_before.astype(jnp.int32) + has_after.astype(jnp.int32)
    mine = inst - 3 * lax.rem(cell, 2)
    busy = jnp.logical_and(mine >= 0, mine < COMP)

    def at(c, i):
        return {"cell": c, "inst": i}

    load = [
        pltpu.make_async_copy(a, b, s_in.at[j])
        for j, (a, b) in enumerate(
            (
                (initial_in, initial),
                (source_in, source),
                (neighbors_in, neighbors),
                (weights_in, weights),
                (damping_in, damping),
            )
        )
    ]
    for copy in load:
        copy.start()

    barrier = pltpu.get_barrier_semaphore()

    def greet(c, i):
        pl.semaphore_signal(barrier, inc=1, device_id=at(c, i), device_id_type=MESH)

    @pl.when(busy)
    def _():
        for j in range(1, GROUP):
            greet(cell, lax.rem(inst + j, GROUP))
        for has, c in ((has_before, before), (has_after, after)):

            @pl.when(has)
            def _():
                for i in range(GROUP):
                    greet(c, i)

    @pl.when(jnp.logical_not(busy))
    def _():
        for v in range(COMP):
            greet(cell, owner(v, cell))

    for which, ref in enumerate((initial, source)):
        load[which].wait()
        for n in range(PER):
            for v in range(COMP):
                x = ref[pl.ds(n * COMP + v, 1), :].reshape(OWN, LANES)
                sx[v, which, n] = x
                sl[v, which, n] = x[OWN - RIM :]
                sr[v, which, n] = x[:RIM]

    for copy in load[2:]:
        copy.wait()
    w = [weights[pl.ds(k, 1), :].reshape(OWN, LANES) for k in range(NEIGH)]
    off = [neighbors[pl.ds(k, 1), :].reshape(OWN, LANES) for k in range(NEIGH)]
    m = RELAX / (damping[...] + ((w[0] + w[1]) + (w[2] + w[3])))
    scale[WIDE : WIDE + OWN] = m
    stl[2 * NEIGH], str_[2 * NEIGH] = m[OWN - RIM :], m[:RIM]
    for k in range(NEIGH):
        g = w[k] * m
        position = lax.broadcasted_iota(jnp.int32, (OWN, LANES), 1) + off[k]
        lane[k, WIDE : WIDE + OWN] = position & (LANES - 1)
        step[k, WIDE : WIDE + OWN] = position >> 7
        gain[k, WIDE : WIDE + OWN] = g
        f = off[k].astype(jnp.float32)
        stl[k], str_[k] = f[OWN - RIM :], f[:RIM]
        stl[NEIGH + k], str_[NEIGH + k] = g[OWN - RIM :], g[:RIM]

    @pl.when(busy)
    def _():
        pl.semaphore_wait(barrier, GROUP - 1 + COMP * sides)

    @pl.when(jnp.logical_not(busy))
    def _():
        pl.semaphore_wait(barrier, COMP + COMP * sides)

    def remote(a, b, s, r, c, i):
        return pltpu.make_async_remote_copy(
            src_ref=a, dst_ref=b, send_sem=s, recv_sem=r, device_id=at(c, i), device_id_type=MESH
        )

    own_copy = [
        remote(sx.at[v], ro.at[inst], s_own.at[v], r_own.at[inst], cell, owner(v, cell)) for v in range(COMP)
    ]
    left_copy = [
        remote(sl.at[v], rl.at[inst], s_left.at[v], r_left.at[inst], after, owner(v, after)) for v in range(COMP)
    ]
    right_copy = [
        remote(sr.at[v], rr.at[inst], s_right.at[v], r_right.at[inst], before, owner(v, before)) for v in range(COMP)
    ]
    @pl.when(has_after)
    def _():
        for v in range(COMP):
            left_copy[v].start()

    @pl.when(has_before)
    def _():
        for v in range(COMP):
            right_copy[v].start()

    for v in range(COMP):

        @pl.when(mine != v)
        def _():
            own_copy[v].start()

    @pl.when(busy)
    def _():
        stat = [
            remote(stl, rstl, s_stat.at[0], r_stat.at[0], after, owner(mine, after)),
            remote(str_, rstr, s_stat.at[1], r_stat.at[1], before, owner(mine, before)),
        ]
        keep = pltpu.make_async_copy(sx.at[mine], ro.at[inst], r_own.at[inst])
        keep.start()

        @pl.when(has_after)
        def _():
            stat[0].start()

        @pl.when(has_before)
        def _():
            stat[1].start()

        def arrived(ref, sem):
            for j in range(GROUP):
                pltpu.make_async_copy(ref.at[j], ref.at[j], sem.at[j]).wait()

        @pl.when(has_before)
        def _():
            stat[0].wait_recv()
            arrived(rl, r_left)

        @pl.when(first)
        def _():
            rl[...] = jnp.zeros_like(rl)
            rstl[...] = jnp.zeros_like(rstl)
            low2[:, :WIDE] = jnp.zeros((LOW, WIDE, LANES), jnp.float32)

        @pl.when(has_after)
        def _():
            stat[1].wait_recv()
            arrived(rr, r_right)

        @pl.when(last)
        def _():
            rr[...] = jnp.zeros_like(rr)
            rstr[...] = jnp.zeros_like(rstr)
            low2[:, WIDE + OWN :] = jnp.zeros((LOW, WIDE, LANES), jnp.float32)

        for start, got in ((WIDE - RIM, rstl), (WIDE + OWN, rstr)):
            rows = pl.ds(start, RIM)
            for k in range(NEIGH):
                position = lax.broadcasted_iota(jnp.int32, (RIM, LANES), 1) + got[k].astype(jnp.int32)
                lane[k, rows] = position & (LANES - 1)
                step[k, rows] = position >> 7
                gain[k, rows] = got[NEIGH + k]
            scale[rows] = got[2 * NEIGH]

        def transform(ref, first, rows, to):
            for which, dst in ((0, u0), (1, src)):
                h = forward([ref[n // PER, which, n % PER, pl.ds(first, rows)] for n in range(NI)])
                for j in range(NI):
                    dst[j, pl.ds(to, rows)] = h[j]

        transform(rl, 0, RIM, WIDE - RIM)
        transform(rr, 0, RIM, WIDE + OWN)
        arrived(ro, r_own)
        for t in range(OWN // 8):
            transform(ro, 8 * t, 8, WIDE + 8 * t)

        def sweep(old, new, start, to, harmonics):
            rows = pl.ds(start, 8)
            lanes = [lane[k, rows] for k in range(NEIGH)]
            steps = [step[k, rows] for k in range(NEIGH)]
            near = [steps[k] == 0 for k in range(NEIGH)]
            next_ = [steps[k] == (1 if k % 2 else -1) for k in range(NEIGH)]
            gains = [gain[k, rows] for k in range(NEIGH)]
            m = scale[rows]

            def coupled(j):
                x = {d: old[j, pl.ds(start + d, 8)] for d in (-2, -1, 0, 1, 2)}
                total = x[0] * (1.0 - RELAX)
                for k in range(NEIGH):
                    sign = 1 if k % 2 else -1
                    pick = [jnp.take_along_axis(x[sign * d], lanes[k], axis=1, mode="promise_in_bounds") for d in range(3)]
                    total = total + gains[k] * jnp.where(near[k], pick[0], jnp.where(next_[k], pick[1], pick[2]))
                return x[0], total

            for k in harmonics:
                if k in (0, 8):
                    j = max(2 * k - 1, 0)
                    _, total = coupled(j)
                    new[j, pl.ds(to, 8)] = total + m * src[j, rows]
                else:
                    a, b = 2 * k - 1, 2 * k
                    xa, ta = coupled(a)
                    xb, tb = coupled(b)
                    new[a, pl.ds(to, 8)] = ta + m * (src[a, rows] - (FREQ * k) * xb)
                    new[b, pl.ds(to, 8)] = tb + m * (src[b, rows] + (FREQ * k) * xa)

        low, high = (0, 1), tuple(range(2, 9))
        for start in (6, 14, 18):
            sweep(u0, u1, start, start, low)
        for start in (8, 16):
            sweep(u1, low2, start, start, low)
        wide = [
            remote(low2.at[:, pl.ds(OWN, WIDE)], low2.at[:, pl.ds(0, WIDE)], s_low.at[0], r_low.at[0], after, owner(mine, after)),
            remote(low2.at[:, pl.ds(WIDE, WIDE)], low2.at[:, pl.ds(WIDE + OWN, WIDE)], s_low.at[1], r_low.at[1], before, owner(mine, before)),
        ]

        @pl.when(has_after)
        def _():
            wide[0].start()

        @pl.when(has_before)
        def _():
            wide[1].start()

        for start in (6, 14, 18):
            sweep(u0, u1, start, start, high)
        for start in (8, 16):
            sweep(u1, fin, start, start - WIDE, high)

        @pl.when(has_before)
        def _():
            wide[0].wait_recv()

        @pl.when(has_after)
        def _():
            wide[1].wait_recv()

        for start in (4, 12, 20):
            sweep(low2, low3, start, start, low)
        for start in (6, 14, 18):
            sweep(low3, low4, start, start, low)
        for start in (8, 16):
            sweep(low4, fin, start, start - WIDE, low)
        for t in range(OWN // 8):
            rows = pl.ds(8 * t, 8)
            x = backward([fin[j, rows] for j in range(NI)])
            for n in range(NI):
                back[n // PER, n % PER, rows] = x[n]
        home = [
            remote(back.at[i], out.at[:, mine], s_out.at[i], r_out.at[mine], cell, i) for i in range(GROUP)
        ]
        for i in range(GROUP):

            @pl.when(inst != i)
            def _():
                home[i].start()

        stay = pltpu.make_async_copy(back.at[inst], out.at[:, mine], r_out.at[mine])
        stay.start()
        for i in range(GROUP):

            @pl.when(inst != i)
            def _():
                home[i].wait_send()

        @pl.when(has_after)
        def _():
            wide[0].wait_send()
            stat[0].wait_send()

        @pl.when(has_before)
        def _():
            wide[1].wait_send()
            stat[1].wait_send()

    @pl.when(has_after)
    def _():
        for v in range(COMP):
            left_copy[v].wait_send()

    @pl.when(has_before)
    def _():
        for v in range(COMP):
            right_copy[v].wait_send()

    for v in range(COMP):

        @pl.when(mine != v)
        def _():
            own_copy[v].wait_send()

    for v in range(COMP):
        pltpu.make_async_copy(out.at[:, v], out.at[:, v], r_out.at[v]).wait()


def per_device(initial, source, neighbors, face_weights, damping):
    vmem = pl.BlockSpec(memory_space=pltpu.VMEM)
    f32, i32 = jnp.float32, jnp.int32
    dma = pltpu.SemaphoreType.DMA
    tall = (NI, ROWS, LANES)
    low = (LOW, ROWS, LANES)
    result = pl.pallas_call(
        kernel,
        out_shape=jax.ShapeDtypeStruct((PER, COMP, OWN, LANES), f32),
        in_specs=[pl.BlockSpec(memory_space=pltpu.HBM)] * 5,
        out_specs=vmem,
        scratch_shapes=[
            pltpu.VMEM((PER * COMP, OWN * LANES), f32),
            pltpu.VMEM((PER * COMP, OWN * LANES), f32),
            pltpu.VMEM((NEIGH, OWN * LANES), i32),
            pltpu.VMEM((NEIGH, OWN * LANES), f32),
            pltpu.VMEM((OWN, LANES), f32),
            pltpu.VMEM((COMP, 2, PER, OWN, LANES), f32),
            pltpu.VMEM((COMP, 2, PER, RIM, LANES), f32),
            pltpu.VMEM((COMP, 2, PER, RIM, LANES), f32),
            pltpu.VMEM((2 * NEIGH + 1, RIM, LANES), f32),
            pltpu.VMEM((2 * NEIGH + 1, RIM, LANES), f32),
            pltpu.VMEM((GROUP, 2, PER, OWN, LANES), f32),
            pltpu.VMEM((GROUP, 2, PER, RIM, LANES), f32),
            pltpu.VMEM((GROUP, 2, PER, RIM, LANES), f32),
            pltpu.VMEM((2 * NEIGH + 1, RIM, LANES), f32),
            pltpu.VMEM((2 * NEIGH + 1, RIM, LANES), f32),
            pltpu.VMEM((NEIGH, ROWS, LANES), i32),
            pltpu.VMEM((NEIGH, ROWS, LANES), i32),
            pltpu.VMEM((NEIGH, ROWS, LANES), f32),
            pltpu.VMEM((ROWS, LANES), f32),
            pltpu.VMEM(tall, f32),
            pltpu.VMEM(tall, f32),
            pltpu.VMEM(tall, f32),
            pltpu.VMEM(low, f32),
            pltpu.VMEM(low, f32),
            pltpu.VMEM(low, f32),
            pltpu.VMEM((NI, OWN, LANES), f32),
            pltpu.VMEM((GROUP, PER, OWN, LANES), f32),
            dma((5,)), dma((COMP,)), dma((COMP,)), dma((COMP,)), dma((2,)),
            dma((GROUP,)), dma((GROUP,)), dma((GROUP,)), dma((2,)),
            dma((2,)), dma((2,)), dma((GROUP,)), dma((COMP,)),
        ],
        compiler_params=pltpu.CompilerParams(
            collective_id=0, has_side_effects=True, vmem_limit_bytes=56 * 1024 * 1024
        ),
    )(initial, source, neighbors, face_weights, damping.reshape(OWN, LANES))
    return result.reshape(PER * COMP, OWN * LANES)


def solution(mesh):
    return jax.shard_map(
        per_device,
        mesh=mesh,
        in_specs=(
            P("inst", "cell"),
            P("inst", "cell"),
            P(None, "cell"),
            P(None, "cell"),
            P("cell"),
        ),
        out_specs=P("inst", "cell"),
        check_vma=False,
    )
```

```python
import math

import jax
import jax.numpy as jnp
from jax import lax
from jax.experimental import pallas as pl
from jax.experimental.pallas import tpu as pltpu
from jax.sharding import PartitionSpec as P

NI = 16
COMP = 5
NEIGH = 4
FREQ = 0.15
RELAX = 0.6
LANES = 128
OWN = 16
SWEEPS_FINE = 2
SWEEPS = 5
REACH = 2
RIM = SWEEPS * REACH
RIM_S = RIM - REACH
ROWS = OWN + 2 * RIM
GROUP = 8
PER = NI // GROUP
MESSAGE = PER * (RIM + RIM_S) + 4
OWNERS = (0, 1, 2, 4, 6)
MESH = pl.DeviceIdType.MESH
ROOT = math.sqrt(0.5)


def forward(x):
    out = [None] * NI
    p = [x[n] + x[n + 8] for n in range(8)]
    q = [x[n] - x[n + 8] for n in range(8)]
    q0, q4 = q[0] * 0.125, q[4] * 0.125
    d = [None] + [q[n] - q[8 - n] for n in (1, 2, 3)]
    s = [None] + [q[n] + q[8 - n] for n in (1, 2, 3)]
    for k in (1, 3, 5, 7):
        a, b = q0, (q4 if k in (1, 5) else -q4)
        for n in (1, 2, 3):
            a = a + d[n] * (math.cos(math.pi * k * n / 8) / 8)
            b = b + s[n] * (math.sin(math.pi * k * n / 8) / 8)
        out[2 * k - 1], out[2 * k] = a, b
    pp = [p[n] + p[n + 4] for n in range(4)]
    pq = [p[n] - p[n + 4] for n in range(4)]
    a, b = pq[0] * 0.125, pq[2] * 0.125
    d1, s1 = (pq[1] - pq[3]) * (ROOT / 8), (pq[1] + pq[3]) * (ROOT / 8)
    out[3], out[4] = a + d1, s1 + b
    out[11], out[12] = a - d1, s1 - b
    out[7], out[8] = (pp[0] - pp[2]) * 0.125, (pp[1] - pp[3]) * 0.125
    even, odd = (pp[0] + pp[2]) * 0.0625, (pp[1] + pp[3]) * 0.0625
    out[0], out[15] = even + odd, even - odd
    return out


def backward(h):
    a = {k: h[2 * k - 1] for k in range(1, 9)}
    a[0] = h[0]
    b = {k: h[2 * k] for k in range(1, 8)}
    odd = [None] * 8
    odd[0] = (a[1] + a[3]) + (a[5] + a[7])
    odd[4] = (b[1] - b[3]) + (b[5] - b[7])
    for n in (1, 2, 3):
        c = s = 0.0
        for k in (1, 3, 5, 7):
            c = c + a[k] * math.cos(math.pi * k * n / 8)
            s = s + b[k] * math.sin(math.pi * k * n / 8)
        odd[n], odd[8 - n] = s + c, s - c
    d, s = (a[2] - a[6]) * ROOT, (b[2] + b[6]) * ROOT
    half = [a[2] + a[6], s + d, b[2] - b[6], s - d]
    up, down = a[0] + a[8], a[0] - a[8]
    quarter = [up + a[4], down + b[4], up - a[4], down - b[4]]
    even = [quarter[n] + half[n] for n in range(4)] + [quarter[n] - half[n] for n in range(4)]
    return [even[n] + odd[n] for n in range(8)] + [even[n] - odd[n] for n in range(8)]


def tiles(start, stop):
    return [min(row, stop - 8) for row in range(start, stop, 8)]


def kernel(
    initial_in, source_in, neighbors_in, weights_in, damping_in, out,
    initial, source, neighbors, weights, damping,
    sx, sl, sr, stl, str_, ro, rl, rr, rstl, rstr,
    lane, step, gain, scale, even, odd, src, fin, back,
    s_in, s_own, s_left, s_right, s_stat, r_own, r_left, r_right, r_stat, s_out, r_out,
):
    cell, inst = lax.axis_index("cell"), lax.axis_index("inst")
    count = lax.axis_size("cell")
    first, last = cell == 0, cell == count - 1
    has_before, has_after = jnp.logical_not(first), jnp.logical_not(last)
    after, before = jnp.minimum(cell + 1, count - 1), jnp.maximum(cell - 1, 0)
    sides = has_before.astype(jnp.int32) + has_after.astype(jnp.int32)
    mine, owns = 0, 0
    for v in range(COMP):
        here = (inst == OWNERS[v]).astype(jnp.int32)
        mine, owns = mine + v * here, owns + here
    busy = owns == 1
    idle = jnp.logical_not(busy)

    load = [
        pltpu.make_async_copy(a, b, s_in.at[j])
        for j, (a, b) in enumerate(
            (
                (initial_in, initial),
                (source_in, source),
                (neighbors_in, neighbors),
                (weights_in, weights),
                (damping_in, damping),
            )
        )
    ]
    for copy in load:
        copy.start()

    barrier = pltpu.get_barrier_semaphore()

    def greet(c, i):
        pl.semaphore_signal(barrier, inc=1, device_id={"cell": c, "inst": i}, device_id_type=MESH)

    @pl.when(busy)
    def _():
        for has, c in ((has_before, before), (has_after, after)):

            @pl.when(has)
            def _():
                for i in range(GROUP):
                    greet(c, i)

        for j in range(1, GROUP):
            greet(cell, lax.rem(inst + j, GROUP))

    for which, ref in enumerate((initial, source)):
        load[which].wait()
        for n in range(PER):
            for v in range(COMP):
                x = ref[pl.ds(n * COMP + v, 1), :].reshape(OWN, LANES)
                sx[v, which, n] = x
                size = (RIM, RIM_S)[which]
                rows = pl.ds((n * RIM, PER * RIM + n * RIM_S)[which], size)
                sl[v, rows] = x[OWN - size :]
                sr[v, rows] = x[:size]

    pl.semaphore_wait(barrier, COMP * (1 + sides) - owns)

    def remote(a, b, s, r, c, i):
        return pltpu.make_async_remote_copy(
            src_ref=a, dst_ref=b, send_sem=s, recv_sem=r, device_id={"cell": c, "inst": i}, device_id_type=MESH
        )

    own_copy = [remote(sx.at[v], ro.at[inst], s_own, r_own, cell, OWNERS[v]) for v in range(COMP)]
    left_copy = [remote(sl.at[v], rl.at[inst], s_left, r_left, after, OWNERS[v]) for v in range(COMP)]
    right_copy = [remote(sr.at[v], rr.at[inst], s_right, r_right, before, OWNERS[v]) for v in range(COMP)]

    for v in range(COMP):

        @pl.when(mine + COMP * (1 - owns) != v)
        def _():
            own_copy[v].start()

    @pl.when(has_after)
    def _():
        for v in range(COMP):
            left_copy[v].start()

    @pl.when(has_before)
    def _():
        for v in range(COMP):
            right_copy[v].start()

    @pl.when(busy)
    def _():
        for copy in load[2:]:
            copy.wait()
        w = [weights[pl.ds(k, 1), :].reshape(OWN, LANES) for k in range(NEIGH)]
        off = [neighbors[pl.ds(k, 1), :].reshape(OWN, LANES) for k in range(NEIGH)]
        m = RELAX / (damping[...] + ((w[0] + w[1]) + (w[2] + w[3])))
        own = pl.ds(RIM, OWN)
        scale[own] = m
        stl[2 * NEIGH], str_[2 * NEIGH] = m[OWN - RIM_S :], m[:RIM_S]
        for k in range(NEIGH):
            g = w[k] * m
            position = lax.broadcasted_iota(jnp.int32, (OWN, LANES), 1) + off[k]
            lane[k, own] = position & (LANES - 1)
            step[k, own] = position >> 7
            gain[k, own] = g
            f = off[k].astype(jnp.float32)
            stl[k], str_[k] = f[OWN - RIM_S :], f[:RIM_S]
            stl[NEIGH + k], str_[NEIGH + k] = g[OWN - RIM_S :], g[:RIM_S]
        stat = [
            remote(stl, rstl, s_stat.at[0], r_stat.at[0], after, inst),
            remote(str_, rstr, s_stat.at[1], r_stat.at[1], before, inst),
        ]

        @pl.when(has_after)
        def _():
            stat[0].start()

        @pl.when(has_before)
        def _():
            stat[1].start()

        ro[inst] = sx[mine]

        @pl.when(has_before)
        def _():
            stat[0].wait_recv()

        @pl.when(first)
        def _():
            rl[...] = jnp.zeros_like(rl)
            rstl[...] = jnp.zeros_like(rstl)

        @pl.when(has_after)
        def _():
            stat[1].wait_recv()

        @pl.when(last)
        def _():
            rr[...] = jnp.zeros_like(rr)
            rstr[...] = jnp.zeros_like(rstr)

        for start, got in ((RIM - RIM_S, rstl), (RIM + OWN, rstr)):
            rows = pl.ds(start, RIM_S)
            for k in range(NEIGH):
                position = lax.broadcasted_iota(jnp.int32, (RIM_S, LANES), 1) + got[k].astype(jnp.int32)
                lane[k, rows] = position & (LANES - 1)
                step[k, rows] = position >> 7
                gain[k, rows] = got[NEIGH + k]
            scale[rows] = got[2 * NEIGH]

        def transform(read, rows, dst, to):
            h = forward([read(n) for n in range(NI)])
            for j in range(NI):
                dst[j, pl.ds(to, rows)] = h[j]

        def rim(ref, which, row, rows):
            base = (0, PER * RIM)[which] + row
            size = (RIM, RIM_S)[which]
            return lambda n: ref[n // PER, pl.ds(base + (n % PER) * size, rows)]

        def all_of(ref, sem):
            pltpu.make_async_copy(ref, ref, sem).wait()

        @pl.when(has_before)
        def _():
            all_of(rl, r_left)

        transform(rim(rl, 0, 0, 2), 2, even, 0)
        transform(rim(rl, 0, 2, 8), 8, even, 2)
        transform(rim(rl, 1, 0, 8), 8, src, 2)

        @pl.when(has_after)
        def _():
            all_of(rr, r_right)

        transform(rim(rr, 0, 8, 2), 2, even, RIM + OWN + 8)
        transform(rim(rr, 0, 0, 8), 8, even, RIM + OWN)
        transform(rim(rr, 1, 0, 8), 8, src, RIM + OWN)
        all_of(ro.at[pl.ds(1, GROUP - 1)], r_own)
        for t in range(0, OWN, 8):
            for which, dst in ((0, even), (1, src)):
                transform(lambda n: ro[n // PER, which, n % PER, pl.ds(t, 8)], 8, dst, RIM + t)

        def sweep(old, new, start, to, harmonics):
            rows = pl.ds(start, 8)
            m = scale[rows]
            names = [j for k in harmonics for j in ((2 * k - 1, 2 * k) if 0 < k < 8 else (max(2 * k - 1, 0),))]
            total = {}
            for k in harmonics:
                if k in (0, 8):
                    j = max(2 * k - 1, 0)
                    total[j] = (1.0 - RELAX) * old[j, rows] + m * src[j, rows]
                else:
                    a, b = 2 * k - 1, 2 * k
                    xa, xb = old[a, rows], old[b, rows]
                    total[a] = (1.0 - RELAX) * xa + m * (src[a, rows] - (FREQ * k) * xb)
                    total[b] = (1.0 - RELAX) * xb + m * (src[b, rows] + (FREQ * k) * xa)
            for k in range(NEIGH):
                sign = 1 if k % 2 else -1
                index, by, g = lane[k, rows], step[k, rows], gain[k, rows]
                near, next_ = by == 0, by == sign
                for j in names:
                    pick = [
                        jnp.take_along_axis(old[j, pl.ds(start + sign * d, 8)], index, axis=1, mode="promise_in_bounds")
                        for d in range(REACH + 1)
                    ]
                    total[j] = total[j] + g * jnp.where(near, pick[0], jnp.where(next_, pick[1], pick[2]))
            for j in names:
                new[j, pl.ds(to, 8)] = total[j]

        low, high = (0, 1), tuple(range(2, 9))
        buffers = (even, odd)
        for harmonics, sweeps in ((low, SWEEPS), (high, SWEEPS_FINE)):
            for s in range(sweeps):
                wide = (sweeps - 1 - s) * REACH
                old, new = buffers[s % 2], buffers[(s + 1) % 2]
                for start in tiles(RIM - wide, RIM + OWN + wide):
                    if s < sweeps - 1:
                        sweep(old, new, start, start, harmonics)
                    else:
                        sweep(old, fin, start, start - RIM, harmonics)
        for t in range(0, OWN, 8):
            rows = pl.ds(t, 8)
            x = backward([fin[j, rows] for j in range(NI)])
            for n in range(NI):
                back[n // PER, n % PER, rows] = x[n]
        home = [remote(back.at[i], out.at[:, mine], s_out, r_out, cell, i) for i in range(GROUP)]
        for i in range(GROUP):

            @pl.when(inst != i)
            def _():
                home[i].start()

        out[:, mine] = back[inst]
        all_of(back.at[pl.ds(1, GROUP - 1)], s_out)

        @pl.when(has_after)
        def _():
            stat[0].wait_send()

        @pl.when(has_before)
        def _():
            stat[1].wait_send()

        all_of(sx.at[pl.ds(1, COMP - 1)], s_own)
        all_of(out.at[:, pl.ds(1, COMP - 1)], r_out)

    @pl.when(idle)
    def _():
        for copy in load[2:]:
            copy.wait()
        pltpu.make_async_copy(sx, sx, s_own).wait()
        pltpu.make_async_copy(out, out, r_out).wait()

    @pl.when(has_after)
    def _():
        pltpu.make_async_copy(sl, sl, s_left).wait()

    @pl.when(has_before)
    def _():
        pltpu.make_async_copy(sr, sr, s_right).wait()


def per_device(initial, source, neighbors, face_weights, damping):
    vmem = pl.BlockSpec(memory_space=pltpu.VMEM)
    f32, i32 = jnp.float32, jnp.int32
    dma = pltpu.SemaphoreType.DMA
    arguments = (initial, source, neighbors, face_weights, damping.reshape(OWN, LANES))
    result = pl.pallas_call(
        kernel,
        out_shape=pltpu.VMEM((PER, COMP, OWN, LANES), f32),
        in_specs=[pl.BlockSpec(memory_space=pltpu.HBM)] * 5,
        out_specs=vmem,
        scratch_shapes=[
            pltpu.VMEM((PER * COMP, OWN * LANES), f32),
            pltpu.VMEM((PER * COMP, OWN * LANES), f32),
            pltpu.VMEM((NEIGH, OWN * LANES), i32),
            pltpu.VMEM((NEIGH, OWN * LANES), f32),
            pltpu.VMEM((OWN, LANES), f32),
            pltpu.VMEM((COMP, 2, PER, OWN, LANES), f32),
            pltpu.VMEM((COMP, MESSAGE, LANES), f32),
            pltpu.VMEM((COMP, MESSAGE, LANES), f32),
            pltpu.VMEM((2 * NEIGH + 1, RIM_S, LANES), f32),
            pltpu.VMEM((2 * NEIGH + 1, RIM_S, LANES), f32),
            pltpu.VMEM((GROUP, 2, PER, OWN, LANES), f32),
            pltpu.VMEM((GROUP, MESSAGE, LANES), f32),
            pltpu.VMEM((GROUP, MESSAGE, LANES), f32),
            pltpu.VMEM((2 * NEIGH + 1, RIM_S, LANES), f32),
            pltpu.VMEM((2 * NEIGH + 1, RIM_S, LANES), f32),
            pltpu.VMEM((NEIGH, ROWS, LANES), i32),
            pltpu.VMEM((NEIGH, ROWS, LANES), i32),
            pltpu.VMEM((NEIGH, ROWS, LANES), f32),
            pltpu.VMEM((ROWS, LANES), f32),
            pltpu.VMEM((NI, ROWS, LANES), f32),
            pltpu.VMEM((NI, ROWS, LANES), f32),
            pltpu.VMEM((NI, ROWS, LANES), f32),
            pltpu.VMEM((NI, OWN, LANES), f32),
            pltpu.VMEM((GROUP, PER, OWN, LANES), f32),
            dma((5,)), dma, dma, dma, dma((2,)), dma, dma, dma, dma((2,)), dma, dma,
        ],
        compiler_params=pltpu.CompilerParams(
            collective_id=0, has_side_effects=True, vmem_limit_bytes=32 * 1024 * 1024
        ),
    )(*(pltpu.with_memory_space_constraint(x, pltpu.HBM) for x in arguments))
    return result.reshape(PER * COMP, OWN * LANES)


def solution(mesh):
    return jax.shard_map(
        per_device,
        mesh=mesh,
        in_specs=(
            P("inst", "cell"),
            P("inst", "cell"),
            P(None, "cell"),
            P(None, "cell"),
            P("cell"),
        ),
        out_specs=P("inst", "cell"),
        check_vma=False,
    )
```

```python
import math

import jax
import jax.numpy as jnp
from jax import lax
from jax.experimental import pallas as pl
from jax.experimental.pallas import tpu as pltpu
from jax.sharding import PartitionSpec as P

NI = 16
COMP = 5
NEIGH = 4
FREQ = 0.15
RELAX = 0.6
LANES = 128
OWN = 16
SWEEPS_FINE = 2
SWEEPS = 5
REACH = 2
RIM = SWEEPS * REACH
RIM_S = RIM - REACH
ROWS = OWN + 2 * RIM
GROUP = 8
PER = NI // GROUP
NEAR = SWEEPS_FINE * REACH
FAR, FAR_S = RIM - NEAR, RIM_S - NEAR
M_NEAR, M_FAR = 16, 24
OWNERS = ((1, 2, 4, 5, 6), (0, 1, 3, 6, 7))
MESH = pl.DeviceIdType.MESH
ROOT = math.sqrt(0.5)


def forward(x):
    out = [None] * NI
    p = [x[n] + x[n + 8] for n in range(8)]
    q = [x[n] - x[n + 8] for n in range(8)]
    q0, q4 = q[0] * 0.125, q[4] * 0.125
    d = [None] + [q[n] - q[8 - n] for n in (1, 2, 3)]
    s = [None] + [q[n] + q[8 - n] for n in (1, 2, 3)]
    for k in (1, 3, 5, 7):
        a, b = q0, (q4 if k in (1, 5) else -q4)
        for n in (1, 2, 3):
            a = a + d[n] * (math.cos(math.pi * k * n / 8) / 8)
            b = b + s[n] * (math.sin(math.pi * k * n / 8) / 8)
        out[2 * k - 1], out[2 * k] = a, b
    pp = [p[n] + p[n + 4] for n in range(4)]
    pq = [p[n] - p[n + 4] for n in range(4)]
    a, b = pq[0] * 0.125, pq[2] * 0.125
    d1, s1 = (pq[1] - pq[3]) * (ROOT / 8), (pq[1] + pq[3]) * (ROOT / 8)
    out[3], out[4] = a + d1, s1 + b
    out[11], out[12] = a - d1, s1 - b
    out[7], out[8] = (pp[0] - pp[2]) * 0.125, (pp[1] - pp[3]) * 0.125
    even, odd = (pp[0] + pp[2]) * 0.0625, (pp[1] + pp[3]) * 0.0625
    out[0], out[15] = even + odd, even - odd
    return out


def forward_low(x):
    p = [x[n] + x[n + 8] for n in range(8)]
    q = [x[n] - x[n + 8] for n in range(8)]
    a, b = q[0] * 0.125, q[4] * 0.125
    for n in (1, 2, 3):
        a = a + (q[n] - q[8 - n]) * (math.cos(math.pi * n / 8) / 8)
        b = b + (q[n] + q[8 - n]) * (math.sin(math.pi * n / 8) / 8)
    return [(((p[0] + p[4]) + (p[2] + p[6])) + ((p[1] + p[5]) + (p[3] + p[7]))) * 0.0625, a, b]


def backward(h):
    a = {k: h[2 * k - 1] for k in range(1, 9)}
    a[0] = h[0]
    b = {k: h[2 * k] for k in range(1, 8)}
    odd = [None] * 8
    odd[0] = (a[1] + a[3]) + (a[5] + a[7])
    odd[4] = (b[1] - b[3]) + (b[5] - b[7])
    for n in (1, 2, 3):
        c = s = 0.0
        for k in (1, 3, 5, 7):
            c = c + a[k] * math.cos(math.pi * k * n / 8)
            s = s + b[k] * math.sin(math.pi * k * n / 8)
        odd[n], odd[8 - n] = s + c, s - c
    d, s = (a[2] - a[6]) * ROOT, (b[2] + b[6]) * ROOT
    half = [a[2] + a[6], s + d, b[2] - b[6], s - d]
    up, down = a[0] + a[8], a[0] - a[8]
    quarter = [up + a[4], down + b[4], up - a[4], down - b[4]]
    even = [quarter[n] + half[n] for n in range(4)] + [quarter[n] - half[n] for n in range(4)]
    return [even[n] + odd[n] for n in range(8)] + [even[n] - odd[n] for n in range(8)]


def tiles(start, stop):
    return [min(row, stop - 8) for row in range(start, stop, 8)]


def kernel(
    initial_in, source_in, neighbors_in, weights_in, damping_in, out,
    initial, source, neighbors, weights, damping,
    sx, sl, sr, fl, fr, stl, str_, ro, rl, rr, gl, gr, rstl, rstr,
    lane, step, gain, scale, even, odd, src, fin, back,
    s_in, s_own, s_left, s_right, s_fl, s_fr, s_stat, r_own, r_left, r_right, r_fl, r_fr, r_stat, s_out, r_out,
):
    cell, inst = lax.axis_index("cell"), lax.axis_index("inst")
    count = lax.axis_size("cell")
    first, last = cell == 0, cell == count - 1
    has_before, has_after = jnp.logical_not(first), jnp.logical_not(last)
    after, before = jnp.minimum(cell + 1, count - 1), jnp.maximum(cell - 1, 0)
    sides = has_before.astype(jnp.int32) + has_after.astype(jnp.int32)
    parity = lax.rem(cell, 2)
    here = [OWNERS[0][v] + parity * (OWNERS[1][v] - OWNERS[0][v]) for v in range(COMP)]
    beside = [OWNERS[1][v] + parity * (OWNERS[0][v] - OWNERS[1][v]) for v in range(COMP)]
    mine, owns, serves = 0, 0, 0
    for v in range(COMP):
        hit = (inst == here[v]).astype(jnp.int32)
        mine, owns = mine + v * hit, owns + hit
        serves = serves + (inst == beside[v]).astype(jnp.int32)
    busy = owns == 1
    idle = jnp.logical_not(busy)

    load = [
        pltpu.make_async_copy(a, b, s_in.at[j])
        for j, (a, b) in enumerate(
            (
                (initial_in, initial),
                (source_in, source),
                (neighbors_in, neighbors),
                (weights_in, weights),
                (damping_in, damping),
            )
        )
    ]
    for copy in load:
        copy.start()

    barrier = pltpu.get_barrier_semaphore()

    def greet(c, i):
        pl.semaphore_signal(barrier, inc=1, device_id={"cell": c, "inst": i}, device_id_type=MESH)

    @pl.when(busy)
    def _():
        for has, c in ((has_before, before), (has_after, after)):

            @pl.when(has)
            def _():
                for i in range(GROUP):
                    greet(c, i)

        for j in range(1, GROUP):
            greet(cell, lax.rem(inst + j, GROUP))

    for copy in load[2:]:
        copy.wait()
    w = [weights[pl.ds(k, 1), :].reshape(OWN, LANES) for k in range(NEIGH)]
    off = [neighbors[pl.ds(k, 1), :].reshape(OWN, LANES) for k in range(NEIGH)]
    m = RELAX / (damping[...] + ((w[0] + w[1]) + (w[2] + w[3])))
    own = pl.ds(RIM, OWN)
    scale[own] = m
    stl[2 * NEIGH], str_[2 * NEIGH] = m[OWN - RIM_S :], m[:RIM_S]
    for k in range(NEIGH):
        g = w[k] * m
        position = lax.broadcasted_iota(jnp.int32, (OWN, LANES), 1) + off[k]
        lane[k, own] = position & (LANES - 1)
        step[k, own] = position >> 7
        gain[k, own] = g
        f = off[k].astype(jnp.float32)
        stl[k], str_[k] = f[OWN - RIM_S :], f[:RIM_S]
        stl[NEIGH + k], str_[NEIGH + k] = g[OWN - RIM_S :], g[:RIM_S]

    pad = jnp.zeros((COMP, M_FAR - PER * (FAR + FAR_S), LANES), jnp.float32)
    fl[:, PER * (FAR + FAR_S) :], fr[:, PER * (FAR + FAR_S) :] = pad, pad

    for which, ref in enumerate((initial, source)):
        load[which].wait()
        for n in range(PER):
            for v in range(COMP):
                x = ref[pl.ds(n * COMP + v, 1), :].reshape(OWN, LANES)
                sx[v, which, n] = x
                rows = pl.ds((which * PER + n) * NEAR, NEAR)
                sl[v, rows], sr[v, rows] = x[OWN - NEAR :], x[:NEAR]
                size = (FAR, FAR_S)[which]
                rows = pl.ds((n * FAR, PER * FAR + n * FAR_S)[which], size)
                fl[v, rows], fr[v, rows] = x[OWN - NEAR - size : OWN - NEAR], x[NEAR : NEAR + size]

    pl.semaphore_wait(barrier, COMP * (1 + sides) - owns)

    def remote(a, b, s, r, c, i):
        return pltpu.make_async_remote_copy(
            src_ref=a, dst_ref=b, send_sem=s, recv_sem=r, device_id={"cell": c, "inst": i}, device_id_type=MESH
        )

    own_copy = [remote(sx.at[v], ro.at[inst], s_own, r_own, cell, here[v]) for v in range(COMP)]
    left_copy = [remote(sl.at[v], rl.at[inst], s_left, r_left, after, beside[v]) for v in range(COMP)]
    right_copy = [remote(sr.at[v], rr.at[inst], s_right, r_right, before, beside[v]) for v in range(COMP)]
    far_left_copy = [remote(fl.at[v], gl.at[inst], s_fl, r_fl, after, beside[v]) for v in range(COMP)]
    far_right_copy = [remote(fr.at[v], gr.at[inst], s_fr, r_fr, before, beside[v]) for v in range(COMP)]
    stat = [
        remote(stl, rstl, s_stat.at[0], r_stat.at[0], after, inst),
        remote(str_, rstr, s_stat.at[1], r_stat.at[1], before, inst),
    ]
    give = [jnp.logical_and(has_after, serves == 1), jnp.logical_and(has_before, serves == 1)]

    for v in range(COMP):

        @pl.when(mine + COMP * (1 - owns) != v)
        def _():
            own_copy[v].start()

    @pl.when(has_after)
    def _():
        for v in range(COMP):
            left_copy[v].start()

    @pl.when(has_before)
    def _():
        for v in range(COMP):
            right_copy[v].start()

    for side in range(2):

        @pl.when(give[side])
        def _():
            stat[side].start()

    @pl.when(has_after)
    def _():
        for v in range(COMP):
            far_left_copy[v].start()

    @pl.when(has_before)
    def _():
        for v in range(COMP):
            far_right_copy[v].start()

    @pl.when(busy)
    def _():
        ro[inst] = sx[mine]

        @pl.when(has_before)
        def _():
            stat[0].wait_recv()

        @pl.when(first)
        def _():
            rl[...] = jnp.zeros_like(rl)
            gl[...] = jnp.zeros_like(gl)
            rstl[...] = jnp.zeros_like(rstl)

        @pl.when(has_after)
        def _():
            stat[1].wait_recv()

        @pl.when(last)
        def _():
            rr[...] = jnp.zeros_like(rr)
            gr[...] = jnp.zeros_like(gr)
            rstr[...] = jnp.zeros_like(rstr)

        for start, got in ((RIM - RIM_S, rstl), (RIM + OWN, rstr)):
            rows = pl.ds(start, RIM_S)
            for k in range(NEIGH):
                position = lax.broadcasted_iota(jnp.int32, (RIM_S, LANES), 1) + got[k].astype(jnp.int32)
                lane[k, rows] = position & (LANES - 1)
                step[k, rows] = position >> 7
                gain[k, rows] = got[NEIGH + k]
            scale[rows] = got[2 * NEIGH]

        def transform(read, rows, dst, to, change=forward):
            h = change([read(n) for n in range(NI)])
            for j in range(len(h)):
                dst[j, pl.ds(to, rows)] = h[j]

        def near(ref, which):
            return lambda n: ref[n // PER, pl.ds((which * PER + n % PER) * NEAR, NEAR)]

        def far(ref, which):
            base, size = (0, PER * FAR)[which], (FAR, FAR_S)[which]
            return lambda n: ref[n // PER, pl.ds(base + (n % PER) * size, size)]

        def all_of(ref, sem):
            pltpu.make_async_copy(ref, ref, sem).wait()

        all_of(ro.at[pl.ds(1, GROUP - 1)], r_own)
        for t in range(0, OWN, 8):
            for which, dst in ((0, even), (1, src)):
                transform(lambda n: ro[n // PER, which, n % PER, pl.ds(t, 8)], 8, dst, RIM + t)

        @pl.when(has_before)
        def _():
            all_of(rl, r_left)

        @pl.when(has_after)
        def _():
            all_of(rr, r_right)

        for which, dst in ((0, even), (1, src)):
            transform(near(rl, which), NEAR, dst, RIM - NEAR)
            transform(near(rr, which), NEAR, dst, RIM + OWN)

        def sweep(old, new, start, to, harmonics):
            rows = pl.ds(start, 8)
            m = scale[rows]
            names = [j for k in harmonics for j in ((2 * k - 1, 2 * k) if 0 < k < 8 else (max(2 * k - 1, 0),))]
            total = {}
            for k in harmonics:
                if k in (0, 8):
                    j = max(2 * k - 1, 0)
                    total[j] = (1.0 - RELAX) * old[j, rows] + m * src[j, rows]
                else:
                    a, b = 2 * k - 1, 2 * k
                    xa, xb = old[a, rows], old[b, rows]
                    total[a] = (1.0 - RELAX) * xa + m * (src[a, rows] - (FREQ * k) * xb)
                    total[b] = (1.0 - RELAX) * xb + m * (src[b, rows] + (FREQ * k) * xa)
            for k in range(NEIGH):
                sign = 1 if k % 2 else -1
                index, by, g = lane[k, rows], step[k, rows], gain[k, rows]
                near, next_ = by == 0, by == sign
                for j in names:
                    pick = [
                        jnp.take_along_axis(old[j, pl.ds(start + sign * d, 8)], index, axis=1, mode="promise_in_bounds")
                        for d in range(REACH + 1)
                    ]
                    total[j] = total[j] + g * jnp.where(near, pick[0], jnp.where(next_, pick[1], pick[2]))
            for j in names:
                new[j, pl.ds(to, 8)] = total[j]

        low, high = (0, 1), tuple(range(2, 9))
        buffers = (even, odd)
        def relax(harmonics, sweeps):
            for s in range(sweeps):
                wide = (sweeps - 1 - s) * REACH
                old, new = buffers[s % 2], buffers[(s + 1) % 2]
                for start in tiles(RIM - wide, RIM + OWN + wide):
                    if s < sweeps - 1:
                        sweep(old, new, start, start, harmonics)
                    else:
                        sweep(old, fin, start, start - RIM, harmonics)

        relax(high, SWEEPS_FINE)

        @pl.when(has_before)
        def _():
            all_of(gl, r_fl)

        @pl.when(has_after)
        def _():
            all_of(gr, r_fr)

        transform(far(gl, 0), FAR, even, 0, forward_low)
        transform(far(gl, 1), FAR_S, src, RIM - RIM_S, forward_low)
        transform(far(gr, 0), FAR, even, RIM + OWN + NEAR, forward_low)
        transform(far(gr, 1), FAR_S, src, RIM + OWN + NEAR, forward_low)
        relax(low, SWEEPS)
        for t in range(0, OWN, 8):
            rows = pl.ds(t, 8)
            x = backward([fin[j, rows] for j in range(NI)])
            for n in range(NI):
                back[n // PER, n % PER, rows] = x[n]
        home = [remote(back.at[i], out.at[:, mine], s_out, r_out, cell, i) for i in range(GROUP)]
        for i in range(GROUP):

            @pl.when(inst != i)
            def _():
                home[i].start()

        out[:, mine] = back[inst]
        all_of(back.at[pl.ds(1, GROUP - 1)], s_out)

        all_of(sx.at[pl.ds(1, COMP - 1)], s_own)
        all_of(out.at[:, pl.ds(1, COMP - 1)], r_out)

    @pl.when(idle)
    def _():
        pltpu.make_async_copy(sx, sx, s_own).wait()
        pltpu.make_async_copy(out, out, r_out).wait()

    for side in range(2):

        @pl.when(give[side])
        def _():
            stat[side].wait_send()

    @pl.when(has_after)
    def _():
        pltpu.make_async_copy(sl, sl, s_left).wait()
        pltpu.make_async_copy(fl, fl, s_fl).wait()

    @pl.when(has_before)
    def _():
        pltpu.make_async_copy(sr, sr, s_right).wait()
        pltpu.make_async_copy(fr, fr, s_fr).wait()


def per_device(initial, source, neighbors, face_weights, damping):
    vmem = pl.BlockSpec(memory_space=pltpu.VMEM)
    f32, i32 = jnp.float32, jnp.int32
    dma = pltpu.SemaphoreType.DMA
    arguments = (initial, source, neighbors, face_weights, damping.reshape(OWN, LANES))
    result = pl.pallas_call(
        kernel,
        out_shape=pltpu.VMEM((PER, COMP, OWN, LANES), f32),
        in_specs=[pl.BlockSpec(memory_space=pltpu.HBM)] * 5,
        out_specs=vmem,
        scratch_shapes=[
            pltpu.VMEM((PER * COMP, OWN * LANES), f32),
            pltpu.VMEM((PER * COMP, OWN * LANES), f32),
            pltpu.VMEM((NEIGH, OWN * LANES), i32),
            pltpu.VMEM((NEIGH, OWN * LANES), f32),
            pltpu.VMEM((OWN, LANES), f32),
            pltpu.VMEM((COMP, 2, PER, OWN, LANES), f32),
            pltpu.VMEM((COMP, M_NEAR, LANES), f32),
            pltpu.VMEM((COMP, M_NEAR, LANES), f32),
            pltpu.VMEM((COMP, M_FAR, LANES), f32),
            pltpu.VMEM((COMP, M_FAR, LANES), f32),
            pltpu.VMEM((2 * NEIGH + 1, RIM_S, LANES), f32),
            pltpu.VMEM((2 * NEIGH + 1, RIM_S, LANES), f32),
            pltpu.VMEM((GROUP, 2, PER, OWN, LANES), f32),
            pltpu.VMEM((GROUP, M_NEAR, LANES), f32),
            pltpu.VMEM((GROUP, M_NEAR, LANES), f32),
            pltpu.VMEM((GROUP, M_FAR, LANES), f32),
            pltpu.VMEM((GROUP, M_FAR, LANES), f32),
            pltpu.VMEM((2 * NEIGH + 1, RIM_S, LANES), f32),
            pltpu.VMEM((2 * NEIGH + 1, RIM_S, LANES), f32),
            pltpu.VMEM((NEIGH, ROWS, LANES), i32),
            pltpu.VMEM((NEIGH, ROWS, LANES), i32),
            pltpu.VMEM((NEIGH, ROWS, LANES), f32),
            pltpu.VMEM((ROWS, LANES), f32),
            pltpu.VMEM((NI, ROWS, LANES), f32),
            pltpu.VMEM((NI, ROWS, LANES), f32),
            pltpu.VMEM((NI, ROWS, LANES), f32),
            pltpu.VMEM((NI, OWN, LANES), f32),
            pltpu.VMEM((GROUP, PER, OWN, LANES), f32),
            dma((5,)), dma, dma, dma, dma, dma, dma((2,)), dma, dma, dma, dma, dma, dma((2,)), dma, dma,
        ],
        compiler_params=pltpu.CompilerParams(
            collective_id=0, has_side_effects=True, vmem_limit_bytes=32 * 1024 * 1024
        ),
    )(*(pltpu.with_memory_space_constraint(x, pltpu.HBM) for x in arguments))
    return result.reshape(PER * COMP, OWN * LANES)


def solution(mesh):
    return jax.shard_map(
        per_device,
        mesh=mesh,
        in_specs=(
            P("inst", "cell"),
            P("inst", "cell"),
            P(None, "cell"),
            P(None, "cell"),
            P("cell"),
        ),
        out_specs=P("inst", "cell"),
        check_vma=False,
    )
```

```python
import math

import jax
import jax.numpy as jnp
from jax import lax
from jax.experimental import pallas as pl
from jax.experimental.pallas import tpu as pltpu
from jax.sharding import PartitionSpec as P

NI = 16
COMP = 5
NEIGH = 4
FREQ = 0.15
RELAX = 0.6
LANES = 128
OWN = 16
SWEEPS_FINE = 2
SWEEPS = 5
REACH = 2
RIM = SWEEPS * REACH
RIM_S = RIM - REACH
ROWS = OWN + 2 * RIM
GROUP = 8
PER = NI // GROUP
NEAR = SWEEPS_FINE * REACH
FAR, FAR_S = RIM - NEAR, RIM_S - NEAR
LOW = 3
M_NEAR, M_FAR = 16, PER * (FAR + FAR_S)
OWNERS = ((1, 2, 3, 4, 5), (0, 1, 4, 6, 7))
MESH = pl.DeviceIdType.MESH
ROOT = math.sqrt(0.5)


def forward(x):
    out = [None] * NI
    p = [x[n] + x[n + 8] for n in range(8)]
    q = [x[n] - x[n + 8] for n in range(8)]
    q0, q4 = q[0] * 0.125, q[4] * 0.125
    d = [None] + [q[n] - q[8 - n] for n in (1, 2, 3)]
    s = [None] + [q[n] + q[8 - n] for n in (1, 2, 3)]
    for k in (1, 3, 5, 7):
        a, b = q0, (q4 if k in (1, 5) else -q4)
        for n in (1, 2, 3):
            a = a + d[n] * (math.cos(math.pi * k * n / 8) / 8)
            b = b + s[n] * (math.sin(math.pi * k * n / 8) / 8)
        out[2 * k - 1], out[2 * k] = a, b
    pp = [p[n] + p[n + 4] for n in range(4)]
    pq = [p[n] - p[n + 4] for n in range(4)]
    a, b = pq[0] * 0.125, pq[2] * 0.125
    d1, s1 = (pq[1] - pq[3]) * (ROOT / 8), (pq[1] + pq[3]) * (ROOT / 8)
    out[3], out[4] = a + d1, s1 + b
    out[11], out[12] = a - d1, s1 - b
    out[7], out[8] = (pp[0] - pp[2]) * 0.125, (pp[1] - pp[3]) * 0.125
    even, odd = (pp[0] + pp[2]) * 0.0625, (pp[1] + pp[3]) * 0.0625
    out[0], out[15] = even + odd, even - odd
    return out


def forward_low(x):
    p = [x[n] + x[n + 8] for n in range(8)]
    q = [x[n] - x[n + 8] for n in range(8)]
    a, b = q[0] * 0.125, q[4] * 0.125
    for n in (1, 2, 3):
        a = a + (q[n] - q[8 - n]) * (math.cos(math.pi * n / 8) / 8)
        b = b + (q[n] + q[8 - n]) * (math.sin(math.pi * n / 8) / 8)
    return [(((p[0] + p[4]) + (p[2] + p[6])) + ((p[1] + p[5]) + (p[3] + p[7]))) * 0.0625, a, b]


def backward(h):
    a = {k: h[2 * k - 1] for k in range(1, 9)}
    a[0] = h[0]
    b = {k: h[2 * k] for k in range(1, 8)}
    odd = [None] * 8
    odd[0] = (a[1] + a[3]) + (a[5] + a[7])
    odd[4] = (b[1] - b[3]) + (b[5] - b[7])
    for n in (1, 2, 3):
        c = s = 0.0
        for k in (1, 3, 5, 7):
            c = c + a[k] * math.cos(math.pi * k * n / 8)
            s = s + b[k] * math.sin(math.pi * k * n / 8)
        odd[n], odd[8 - n] = s + c, s - c
    d, s = (a[2] - a[6]) * ROOT, (b[2] + b[6]) * ROOT
    half = [a[2] + a[6], s + d, b[2] - b[6], s - d]
    up, down = a[0] + a[8], a[0] - a[8]
    quarter = [up + a[4], down + b[4], up - a[4], down - b[4]]
    even = [quarter[n] + half[n] for n in range(4)] + [quarter[n] - half[n] for n in range(4)]
    return [even[n] + odd[n] for n in range(8)] + [even[n] - odd[n] for n in range(8)]


def tiles(start, stop):
    return [min(row, stop - 8) for row in range(start, stop, 8)]


def kernel(
    initial_in, source_in, neighbors_in, weights_in, damping_in, out,
    initial, source, neighbors, weights, damping,
    sx, sn, sf, st_outer, st_flip, ro, rn, rf, got_outer, got_flip, hs, hr,
    lane, step, gain, scale, even, odd, src, fin, back,
    s_in, s_own, s_near, s_far, s_stat, s_rim, r_own, r_near, r_far, r_stat, r_rim, s_out, r_out,
):
    cell, inst = lax.axis_index("cell"), lax.axis_index("inst")
    count = lax.axis_size("cell")
    odd_block = lax.rem(cell, 2)
    is_even = odd_block == 0
    flip = cell + 1 - 2 * odd_block
    beyond = cell - 1 + 2 * odd_block
    has_outer = jnp.logical_and(beyond >= 0, beyond < count)
    outer = jnp.minimum(jnp.maximum(beyond, 0), count - 1)

    def owners(c):
        high = lax.rem(lax.div(c, 2), 2)
        return [OWNERS[0][v] + high * (OWNERS[1][v] - OWNERS[0][v]) for v in range(COMP)]

    here, there = owners(cell), owners(cell + 2)
    mine, owns, serves = 0, 0, 0
    for v in range(COMP):
        hit = (inst == here[v]).astype(jnp.int32)
        mine, owns = mine + v * hit, owns + hit
        serves = serves + (inst == there[v]).astype(jnp.int32)
    busy = owns == 1
    idle = jnp.logical_not(busy)
    give = jnp.logical_and(has_outer, serves == 1)

    load = [
        pltpu.make_async_copy(a, b, s_in.at[j])
        for j, (a, b) in enumerate(
            (
                (initial_in, initial),
                (source_in, source),
                (neighbors_in, neighbors),
                (weights_in, weights),
                (damping_in, damping),
            )
        )
    ]
    for copy in load:
        copy.start()

    barrier = pltpu.get_barrier_semaphore()

    def greet(c, i):
        pl.semaphore_signal(barrier, inc=1, device_id={"cell": c, "inst": i}, device_id_type=MESH)

    @pl.when(busy)
    def _():
        @pl.when(has_outer)
        def _():
            for i in range(GROUP):
                greet(outer, i)

        greet(flip, inst)
        for j in range(1, GROUP):
            greet(cell, lax.rem(inst + j, GROUP))

    for copy in load[2:]:
        copy.wait()
    w = [weights[pl.ds(k, 1), :].reshape(OWN, LANES) for k in range(NEIGH)]
    off = [neighbors[pl.ds(k, 1), :].reshape(OWN, LANES) for k in range(NEIGH)]
    m = RELAX / (damping[...] + ((w[0] + w[1]) + (w[2] + w[3])))
    own = pl.ds(RIM, OWN)
    scale[own] = m

    def edges(k, x):
        head, tail = x[:RIM_S], x[OWN - RIM_S :]
        st_outer[k], st_flip[k] = jnp.where(is_even, head, tail), jnp.where(is_even, tail, head)

    edges(2 * NEIGH, m)
    for k in range(NEIGH):
        g = w[k] * m
        position = lax.broadcasted_iota(jnp.int32, (OWN, LANES), 1) + off[k]
        lane[k, own] = position & (LANES - 1)
        step[k, own] = position >> 7
        gain[k, own] = g
        edges(k, off[k].astype(jnp.float32))
        edges(NEIGH + k, g)

    hs[NI:] = jnp.zeros((2 * LOW, 8, LANES), jnp.float32)

    for which, ref in enumerate((initial, source)):
        load[which].wait()
        for n in range(PER):
            for v in range(COMP):
                x = ref[pl.ds(n * COMP + v, 1), :].reshape(OWN, LANES)
                sx[v, which, n] = x
                near_rows = pl.ds((which * PER + n) * NEAR, NEAR)
                sn[v, near_rows] = jnp.where(is_even, x[:NEAR], x[OWN - NEAR :])
                size = (FAR, FAR_S)[which]
                far_rows = pl.ds((n * FAR, PER * FAR + n * FAR_S)[which], size)
                sf[v, far_rows] = jnp.where(is_even, x[NEAR : NEAR + size], x[OWN - NEAR - size : OWN - NEAR])

    pl.semaphore_wait(barrier, COMP * (1 + has_outer.astype(jnp.int32)))

    def remote(a, b, s, r, c, i):
        return pltpu.make_async_remote_copy(
            src_ref=a, dst_ref=b, send_sem=s, recv_sem=r, device_id={"cell": c, "inst": i}, device_id_type=MESH
        )

    own_copy = [remote(sx.at[v], ro.at[inst], s_own, r_own, cell, here[v]) for v in range(COMP)]
    near_copy = [remote(sn.at[v], rn.at[inst], s_near, r_near, outer, there[v]) for v in range(COMP)]
    far_copy = [remote(sf.at[v], rf.at[inst], s_far, r_far, outer, there[v]) for v in range(COMP)]
    stat_outer = remote(st_outer, got_outer, s_stat.at[0], r_stat.at[0], outer, inst)
    stat_flip = remote(st_flip, got_flip, s_stat.at[1], r_stat.at[1], flip, inst)
    rim_flip = remote(hs, hr, s_rim, r_rim, flip, inst)

    for v in range(COMP):

        @pl.when(mine + COMP * (1 - owns) != v)
        def _():
            own_copy[v].start()

    @pl.when(has_outer)
    def _():
        for v in range(COMP):
            near_copy[v].start()

    @pl.when(give)
    def _():
        stat_outer.start()

    @pl.when(has_outer)
    def _():
        for v in range(COMP):
            far_copy[v].start()

    @pl.when(busy)
    def _():
        stat_flip.start()
        ro[inst] = sx[mine]

        @pl.when(has_outer)
        def _():
            stat_outer.wait_recv()

        @pl.when(jnp.logical_not(has_outer))
        def _():
            rn[...] = jnp.zeros_like(rn)
            rf[...] = jnp.zeros_like(rf)
            got_outer[...] = jnp.zeros_like(got_outer)

        stat_flip.wait_recv()

        def pick(even_row, odd_row):
            return even_row + odd_block * (odd_row - even_row)

        left, right = (RIM - NEAR, 0, FAR - FAR_S), (RIM + OWN, RIM + OWN + NEAR, RIM + OWN + NEAR)
        at_outer = [pick(a, b) for a, b in zip(left, right)]
        at_flip = [pick(b, a) for a, b in zip(left, right)]
        for start, got in (
            (pick(RIM - RIM_S, RIM + OWN), got_outer),
            (pick(RIM + OWN, RIM - RIM_S), got_flip),
        ):
            rows = pl.ds(start, RIM_S)
            for k in range(NEIGH):
                position = lax.broadcasted_iota(jnp.int32, (RIM_S, LANES), 1) + got[k].astype(jnp.int32)
                lane[k, rows] = position & (LANES - 1)
                step[k, rows] = position >> 7
                gain[k, rows] = got[NEIGH + k]
            scale[rows] = got[2 * NEIGH]

        def transform(read, rows, dst, to, change=forward):
            h = change([read(n) for n in range(NI)])
            for j in range(len(h)):
                dst[j, pl.ds(to, rows)] = h[j]

        def near(ref, which):
            return lambda n: ref[n // PER, pl.ds((which * PER + n % PER) * NEAR, NEAR)]

        def far(ref, which):
            base, size = (0, PER * FAR)[which], (FAR, FAR_S)[which]
            return lambda n: ref[n // PER, pl.ds(base + (n % PER) * size, size)]

        def all_of(ref, sem):
            pltpu.make_async_copy(ref, ref, sem).wait()

        all_of(ro.at[pl.ds(1, GROUP - 1)], r_own)
        for t in range(0, OWN, 8):
            for which, dst in ((0, even), (1, src)):
                transform(lambda n: ro[n // PER, which, n % PER, pl.ds(t, 8)], 8, dst, RIM + t)

        to_near, to_far, to_far_s = pick(RIM + OWN - NEAR, RIM), pick(RIM + OWN - RIM, RIM + NEAR), pick(RIM + OWN - RIM_S, RIM + NEAR)
        for j in range(NI):
            hs[j, :NEAR], hs[j, NEAR:] = even[j, pl.ds(to_near, NEAR)], src[j, pl.ds(to_near, NEAR)]
        for j in range(LOW):
            hs[NI + j, :FAR] = even[j, pl.ds(to_far, FAR)]
            hs[NI + LOW + j, :FAR_S] = src[j, pl.ds(to_far_s, FAR_S)]
        rim_flip.start()

        @pl.when(has_outer)
        def _():
            all_of(rn, r_near)

        for which, dst in ((0, even), (1, src)):
            transform(near(rn, which), NEAR, dst, at_outer[0])
        rim_flip.wait_recv()
        for j in range(NI):
            even[j, pl.ds(at_flip[0], NEAR)], src[j, pl.ds(at_flip[0], NEAR)] = hr[j, :NEAR], hr[j, NEAR:]
        for j in range(LOW):
            even[j, pl.ds(at_flip[1], FAR)] = hr[NI + j, :FAR]
            src[j, pl.ds(at_flip[2], FAR_S)] = hr[NI + LOW + j, :FAR_S]

        def sweep(old, new, start, to, harmonics):
            rows = pl.ds(start, 8)
            m = scale[rows]
            names = [j for k in harmonics for j in ((2 * k - 1, 2 * k) if 0 < k < 8 else (max(2 * k - 1, 0),))]
            total = {}
            for k in harmonics:
                if k in (0, 8):
                    j = max(2 * k - 1, 0)
                    total[j] = (1.0 - RELAX) * old[j, rows] + m * src[j, rows]
                else:
                    a, b = 2 * k - 1, 2 * k
                    xa, xb = old[a, rows], old[b, rows]
                    total[a] = (1.0 - RELAX) * xa + m * (src[a, rows] - (FREQ * k) * xb)
                    total[b] = (1.0 - RELAX) * xb + m * (src[b, rows] + (FREQ * k) * xa)
            for k in range(NEIGH):
                sign = 1 if k % 2 else -1
                index, by, g = lane[k, rows], step[k, rows], gain[k, rows]
                near, next_ = by == 0, by == sign
                for j in names:
                    pick = [
                        jnp.take_along_axis(old[j, pl.ds(start + sign * d, 8)], index, axis=1, mode="promise_in_bounds")
                        for d in range(REACH + 1)
                    ]
                    total[j] = total[j] + g * jnp.where(near, pick[0], jnp.where(next_, pick[1], pick[2]))
            for j in names:
                new[j, pl.ds(to, 8)] = total[j]

        low, high = (0, 1), tuple(range(2, 9))
        buffers = (even, odd)
        def relax(harmonics, sweeps):
            for s in range(sweeps):
                wide = (sweeps - 1 - s) * REACH
                old, new = buffers[s % 2], buffers[(s + 1) % 2]
                for start in tiles(RIM - wide, RIM + OWN + wide):
                    if s < sweeps - 1:
                        sweep(old, new, start, start, harmonics)
                    else:
                        sweep(old, fin, start, start - RIM, harmonics)

        relax(high, SWEEPS_FINE)

        @pl.when(has_outer)
        def _():
            all_of(rf, r_far)

        transform(far(rf, 0), FAR, even, at_outer[1], forward_low)
        transform(far(rf, 1), FAR_S, src, at_outer[2], forward_low)
        relax(low, SWEEPS)
        for t in range(0, OWN, 8):
            rows = pl.ds(t, 8)
            x = backward([fin[j, rows] for j in range(NI)])
            for n in range(NI):
                back[n // PER, n % PER, rows] = x[n]
        home = [remote(back.at[i], out.at[:, mine], s_out, r_out, cell, i) for i in range(GROUP)]
        for i in range(GROUP):

            @pl.when(inst != i)
            def _():
                home[i].start()

        out[:, mine] = back[inst]
        all_of(back.at[pl.ds(1, GROUP - 1)], s_out)

        all_of(sx.at[pl.ds(1, COMP - 1)], s_own)
        stat_flip.wait_send()
        rim_flip.wait_send()
        all_of(out.at[:, pl.ds(1, COMP - 1)], r_out)

    @pl.when(idle)
    def _():
        pltpu.make_async_copy(sx, sx, s_own).wait()
        pltpu.make_async_copy(out, out, r_out).wait()

    @pl.when(give)
    def _():
        stat_outer.wait_send()

    @pl.when(has_outer)
    def _():
        pltpu.make_async_copy(sn, sn, s_near).wait()
        pltpu.make_async_copy(sf, sf, s_far).wait()


def per_device(initial, source, neighbors, face_weights, damping):
    vmem = pl.BlockSpec(memory_space=pltpu.VMEM)
    f32, i32 = jnp.float32, jnp.int32
    dma = pltpu.SemaphoreType.DMA
    arguments = (initial, source, neighbors, face_weights, damping.reshape(OWN, LANES))
    result = pl.pallas_call(
        kernel,
        out_shape=pltpu.VMEM((PER, COMP, OWN, LANES), f32),
        in_specs=[pl.BlockSpec(memory_space=pltpu.HBM)] * 5,
        out_specs=vmem,
        scratch_shapes=[
            pltpu.VMEM((PER * COMP, OWN * LANES), f32),
            pltpu.VMEM((PER * COMP, OWN * LANES), f32),
            pltpu.VMEM((NEIGH, OWN * LANES), i32),
            pltpu.VMEM((NEIGH, OWN * LANES), f32),
            pltpu.VMEM((OWN, LANES), f32),
            pltpu.VMEM((COMP, 2, PER, OWN, LANES), f32),
            pltpu.VMEM((COMP, M_NEAR, LANES), f32),
            pltpu.VMEM((COMP, M_FAR, LANES), f32),
            pltpu.VMEM((2 * NEIGH + 1, RIM_S, LANES), f32),
            pltpu.VMEM((2 * NEIGH + 1, RIM_S, LANES), f32),
            pltpu.VMEM((GROUP, 2, PER, OWN, LANES), f32),
            pltpu.VMEM((GROUP, M_NEAR, LANES), f32),
            pltpu.VMEM((GROUP, M_FAR, LANES), f32),
            pltpu.VMEM((2 * NEIGH + 1, RIM_S, LANES), f32),
            pltpu.VMEM((2 * NEIGH + 1, RIM_S, LANES), f32),
            pltpu.VMEM((NI + 2 * LOW, 8, LANES), f32),
            pltpu.VMEM((NI + 2 * LOW, 8, LANES), f32),
            pltpu.VMEM((NEIGH, ROWS, LANES), i32),
            pltpu.VMEM((NEIGH, ROWS, LANES), i32),
            pltpu.VMEM((NEIGH, ROWS, LANES), f32),
            pltpu.VMEM((ROWS, LANES), f32),
            pltpu.VMEM((NI, ROWS, LANES), f32),
            pltpu.VMEM((NI, ROWS, LANES), f32),
            pltpu.VMEM((NI, ROWS, LANES), f32),
            pltpu.VMEM((NI, OWN, LANES), f32),
            pltpu.VMEM((GROUP, PER, OWN, LANES), f32),
            dma((5,)), dma, dma, dma, dma((2,)), dma, dma, dma, dma, dma((2,)), dma, dma, dma,
        ],
        compiler_params=pltpu.CompilerParams(
            collective_id=0, has_side_effects=True, vmem_limit_bytes=32 * 1024 * 1024
        ),
    )(*(pltpu.with_memory_space_constraint(x, pltpu.HBM) for x in arguments))
    return result.reshape(PER * COMP, OWN * LANES)


def solution(mesh):
    return jax.shard_map(
        per_device,
        mesh=mesh,
        in_specs=(
            P("inst", "cell"),
            P("inst", "cell"),
            P(None, "cell"),
            P(None, "cell"),
            P("cell"),
        ),
        out_specs=P("inst", "cell"),
        check_vma=False,
    )
```

```python
import math

import jax
import jax.numpy as jnp
from jax import lax
from jax.experimental import pallas as pl
from jax.experimental.pallas import tpu as pltpu
from jax.sharding import PartitionSpec as P

NI = 16
COMP = 5
NEIGH = 4
FREQ = 0.15
RELAX = 0.6
LANES = 128
OWN = 16
SWEEPS_FINE = 2
SWEEPS = 5
REACH = 2
RIM = SWEEPS * REACH
RIM_S = RIM - REACH
ROWS = OWN + 2 * RIM
GROUP = 8
PER = NI // GROUP
NEAR = SWEEPS_FINE * REACH
FAR, FAR_S = RIM - NEAR, RIM_S - NEAR
LOW = 3
M_NEAR, M_FAR = 16, PER * (FAR + FAR_S)
OWNERS = ((1, 2, 3, 4, 6), (0, 1, 2, 4, 6))
MESH = pl.DeviceIdType.MESH
ROOT = math.sqrt(0.5)


def forward(x):
    out = [None] * NI
    p = [x[n] + x[n + 8] for n in range(8)]
    q = [x[n] - x[n + 8] for n in range(8)]
    q0, q4 = q[0] * 0.125, q[4] * 0.125
    d = [None] + [q[n] - q[8 - n] for n in (1, 2, 3)]
    s = [None] + [q[n] + q[8 - n] for n in (1, 2, 3)]
    for k in (1, 3, 5, 7):
        a, b = q0, (q4 if k in (1, 5) else -q4)
        for n in (1, 2, 3):
            a = a + d[n] * (math.cos(math.pi * k * n / 8) / 8)
            b = b + s[n] * (math.sin(math.pi * k * n / 8) / 8)
        out[2 * k - 1], out[2 * k] = a, b
    pp = [p[n] + p[n + 4] for n in range(4)]
    pq = [p[n] - p[n + 4] for n in range(4)]
    a, b = pq[0] * 0.125, pq[2] * 0.125
    d1, s1 = (pq[1] - pq[3]) * (ROOT / 8), (pq[1] + pq[3]) * (ROOT / 8)
    out[3], out[4] = a + d1, s1 + b
    out[11], out[12] = a - d1, s1 - b
    out[7], out[8] = (pp[0] - pp[2]) * 0.125, (pp[1] - pp[3]) * 0.125
    even, odd = (pp[0] + pp[2]) * 0.0625, (pp[1] + pp[3]) * 0.0625
    out[0], out[15] = even + odd, even - odd
    return out


def forward_low(x):
    p = [x[n] + x[n + 8] for n in range(8)]
    q = [x[n] - x[n + 8] for n in range(8)]
    a, b = q[0] * 0.125, q[4] * 0.125
    for n in (1, 2, 3):
        a = a + (q[n] - q[8 - n]) * (math.cos(math.pi * n / 8) / 8)
        b = b + (q[n] + q[8 - n]) * (math.sin(math.pi * n / 8) / 8)
    return [(((p[0] + p[4]) + (p[2] + p[6])) + ((p[1] + p[5]) + (p[3] + p[7]))) * 0.0625, a, b]


def backward(h):
    a = {k: h[2 * k - 1] for k in range(1, 9)}
    a[0] = h[0]
    b = {k: h[2 * k] for k in range(1, 8)}
    odd = [None] * 8
    odd[0] = (a[1] + a[3]) + (a[5] + a[7])
    odd[4] = (b[1] - b[3]) + (b[5] - b[7])
    for n in (1, 2, 3):
        c = s = 0.0
        for k in (1, 3, 5, 7):
            c = c + a[k] * math.cos(math.pi * k * n / 8)
            s = s + b[k] * math.sin(math.pi * k * n / 8)
        odd[n], odd[8 - n] = s + c, s - c
    d, s = (a[2] - a[6]) * ROOT, (b[2] + b[6]) * ROOT
    half = [a[2] + a[6], s + d, b[2] - b[6], s - d]
    up, down = a[0] + a[8], a[0] - a[8]
    quarter = [up + a[4], down + b[4], up - a[4], down - b[4]]
    even = [quarter[n] + half[n] for n in range(4)] + [quarter[n] - half[n] for n in range(4)]
    return [even[n] + odd[n] for n in range(8)] + [even[n] - odd[n] for n in range(8)]


def tiles(start, stop):
    return [min(row, stop - 8) for row in range(start, stop, 8)]


def kernel(
    initial_in, source_in, neighbors_in, weights_in, damping_in, out,
    initial, source, neighbors, weights, damping,
    sx, sn, sf, st_outer, st_flip, ro, rn, rf, got_outer, got_flip, hs, hr,
    lane, step, gain, scale, even, odd, src, fin, back,
    s_in, s_own, s_near, s_far, s_stat, s_rim, r_own, r_near, r_far, r_stat, r_rim, s_out, r_out,
):
    cell, inst = lax.axis_index("cell"), lax.axis_index("inst")
    count = lax.axis_size("cell")
    odd_block = lax.rem(cell, 2)
    is_even = odd_block == 0
    flip = cell + 1 - 2 * odd_block
    beyond = cell - 1 + 2 * odd_block
    has_outer = jnp.logical_and(beyond >= 0, beyond < count)
    outer = jnp.minimum(jnp.maximum(beyond, 0), count - 1)

    def owners(c):
        high = lax.rem(lax.div(c, 2), 2)
        return [OWNERS[0][v] + high * (OWNERS[1][v] - OWNERS[0][v]) for v in range(COMP)]

    here, there = owners(cell), owners(cell + 2)
    mine, owns, serves = 0, 0, 0
    for v in range(COMP):
        hit = (inst == here[v]).astype(jnp.int32)
        mine, owns = mine + v * hit, owns + hit
        serves = serves + (inst == there[v]).astype(jnp.int32)
    busy = owns == 1
    idle = jnp.logical_not(busy)
    give = jnp.logical_and(has_outer, serves == 1)

    load = [
        pltpu.make_async_copy(a, b, s_in.at[j])
        for j, (a, b) in enumerate(
            (
                (initial_in, initial),
                (source_in, source),
                (neighbors_in, neighbors),
                (weights_in, weights),
                (damping_in, damping),
            )
        )
    ]
    for copy in load:
        copy.start()

    barrier = pltpu.get_barrier_semaphore()

    def greet(c, i):
        pl.semaphore_signal(barrier, inc=1, device_id={"cell": c, "inst": i}, device_id_type=MESH)

    @pl.when(busy)
    def _():
        @pl.when(has_outer)
        def _():
            for i in range(GROUP):
                greet(outer, i)

        greet(flip, inst)
        for j in range(1, GROUP):
            greet(cell, lax.rem(inst + j, GROUP))

    for copy in load[2:]:
        copy.wait()
    w = [weights[pl.ds(k, 1), :].reshape(OWN, LANES) for k in range(NEIGH)]
    off = [neighbors[pl.ds(k, 1), :].reshape(OWN, LANES) for k in range(NEIGH)]
    m = RELAX / (damping[...] + ((w[0] + w[1]) + (w[2] + w[3])))
    own = pl.ds(RIM, OWN)
    scale[own] = m

    def edges(k, x):
        head, tail = x[:RIM_S], x[OWN - RIM_S :]
        st_outer[k], st_flip[k] = jnp.where(is_even, head, tail), jnp.where(is_even, tail, head)

    edges(2 * NEIGH, m)
    for k in range(NEIGH):
        g = w[k] * m
        position = lax.broadcasted_iota(jnp.int32, (OWN, LANES), 1) + off[k]
        lane[k, own] = position & (LANES - 1)
        step[k, own] = position >> 7
        gain[k, own] = g
        edges(k, off[k].astype(jnp.float32))
        edges(NEIGH + k, g)

    hs[NI:] = jnp.zeros((2 * LOW, 8, LANES), jnp.float32)

    for which, ref in enumerate((initial, source)):
        load[which].wait()
        for n in range(PER):
            for v in range(COMP):
                x = ref[pl.ds(n * COMP + v, 1), :].reshape(OWN, LANES)
                sx[v, which, n] = x
                near_rows = pl.ds((which * PER + n) * NEAR, NEAR)
                sn[v, near_rows] = jnp.where(is_even, x[:NEAR], x[OWN - NEAR :])
                size = (FAR, FAR_S)[which]
                far_rows = pl.ds((n * FAR, PER * FAR + n * FAR_S)[which], size)
                sf[v, far_rows] = jnp.where(is_even, x[NEAR : NEAR + size], x[OWN - NEAR - size : OWN - NEAR])

    pl.semaphore_wait(barrier, COMP * (1 + has_outer.astype(jnp.int32)))

    def remote(a, b, s, r, c, i):
        return pltpu.make_async_remote_copy(
            src_ref=a, dst_ref=b, send_sem=s, recv_sem=r, device_id={"cell": c, "inst": i}, device_id_type=MESH
        )

    own_copy = [remote(sx.at[v], ro.at[inst], s_own, r_own, cell, here[v]) for v in range(COMP)]
    near_copy = [remote(sn.at[v], rn.at[inst], s_near, r_near, outer, there[v]) for v in range(COMP)]
    far_copy = [remote(sf.at[v], rf.at[inst], s_far, r_far, outer, there[v]) for v in range(COMP)]
    stat_outer = remote(st_outer, got_outer, s_stat.at[0], r_stat.at[0], outer, inst)
    stat_flip = remote(st_flip, got_flip, s_stat.at[1], r_stat.at[1], flip, inst)
    rim_flip = remote(hs, hr, s_rim, r_rim, flip, inst)

    for v in range(COMP):

        @pl.when(mine + COMP * (1 - owns) != v)
        def _():
            own_copy[v].start()

    @pl.when(has_outer)
    def _():
        for v in range(COMP):
            near_copy[v].start()

    @pl.when(give)
    def _():
        stat_outer.start()

    @pl.when(has_outer)
    def _():
        for v in range(COMP):
            far_copy[v].start()

    @pl.when(busy)
    def _():
        stat_flip.start()
        ro[inst] = sx[mine]

        @pl.when(has_outer)
        def _():
            stat_outer.wait_recv()

        @pl.when(jnp.logical_not(has_outer))
        def _():
            rn[...] = jnp.zeros_like(rn)
            rf[...] = jnp.zeros_like(rf)
            got_outer[...] = jnp.zeros_like(got_outer)

        stat_flip.wait_recv()

        def pick(even_row, odd_row):
            return even_row + odd_block * (odd_row - even_row)

        left, right = (RIM - NEAR, 0, FAR - FAR_S), (RIM + OWN, RIM + OWN + NEAR, RIM + OWN + NEAR)
        at_outer = [pick(a, b) for a, b in zip(left, right)]
        at_flip = [pick(b, a) for a, b in zip(left, right)]
        for start, got in (
            (pick(RIM - RIM_S, RIM + OWN), got_outer),
            (pick(RIM + OWN, RIM - RIM_S), got_flip),
        ):
            rows = pl.ds(start, RIM_S)
            for k in range(NEIGH):
                position = lax.broadcasted_iota(jnp.int32, (RIM_S, LANES), 1) + got[k].astype(jnp.int32)
                lane[k, rows] = position & (LANES - 1)
                step[k, rows] = position >> 7
                gain[k, rows] = got[NEIGH + k]
            scale[rows] = got[2 * NEIGH]

        def transform(read, rows, dst, to, change=forward):
            h = change([read(n) for n in range(NI)])
            for j in range(len(h)):
                dst[j, pl.ds(to, rows)] = h[j]

        def near(ref, which):
            return lambda n: ref[n // PER, pl.ds((which * PER + n % PER) * NEAR, NEAR)]

        def far(ref, which):
            base, size = (0, PER * FAR)[which], (FAR, FAR_S)[which]
            return lambda n: ref[n // PER, pl.ds(base + (n % PER) * size, size)]

        def all_of(ref, sem):
            pltpu.make_async_copy(ref, ref, sem).wait()

        all_of(ro.at[pl.ds(1, GROUP - 1)], r_own)
        for t in range(0, OWN, 8):
            for which, dst in ((0, even), (1, src)):
                transform(lambda n: ro[n // PER, which, n % PER, pl.ds(t, 8)], 8, dst, RIM + t)

        to_near, to_far, to_far_s = pick(RIM + OWN - NEAR, RIM), pick(RIM + OWN - RIM, RIM + NEAR), pick(RIM + OWN - RIM_S, RIM + NEAR)
        for j in range(NI):
            hs[j, :NEAR], hs[j, NEAR:] = even[j, pl.ds(to_near, NEAR)], src[j, pl.ds(to_near, NEAR)]
        for j in range(LOW):
            hs[NI + j, :FAR] = even[j, pl.ds(to_far, FAR)]
            hs[NI + LOW + j, :FAR_S] = src[j, pl.ds(to_far_s, FAR_S)]
        rim_flip.start()

        @pl.when(has_outer)
        def _():
            all_of(rn, r_near)

        for which, dst in ((0, even), (1, src)):
            transform(near(rn, which), NEAR, dst, at_outer[0])
        rim_flip.wait_recv()
        for j in range(NI):
            even[j, pl.ds(at_flip[0], NEAR)], src[j, pl.ds(at_flip[0], NEAR)] = hr[j, :NEAR], hr[j, NEAR:]
        for j in range(LOW):
            even[j, pl.ds(at_flip[1], FAR)] = hr[NI + j, :FAR]
            src[j, pl.ds(at_flip[2], FAR_S)] = hr[NI + LOW + j, :FAR_S]

        def sweep(old, new, start, to, harmonics):
            rows = pl.ds(start, 8)
            m = scale[rows]
            names = [j for k in harmonics for j in ((2 * k - 1, 2 * k) if 0 < k < 8 else (max(2 * k - 1, 0),))]
            total = {}
            for k in harmonics:
                if k in (0, 8):
                    j = max(2 * k - 1, 0)
                    total[j] = (1.0 - RELAX) * old[j, rows] + m * src[j, rows]
                else:
                    a, b = 2 * k - 1, 2 * k
                    xa, xb = old[a, rows], old[b, rows]
                    total[a] = (1.0 - RELAX) * xa + m * (src[a, rows] - (FREQ * k) * xb)
                    total[b] = (1.0 - RELAX) * xb + m * (src[b, rows] + (FREQ * k) * xa)
            for k in range(NEIGH):
                sign = 1 if k % 2 else -1
                index, by, g = lane[k, rows], step[k, rows], gain[k, rows]
                near, next_ = by == 0, by == sign
                for j in names:
                    pick = [
                        jnp.take_along_axis(old[j, pl.ds(start + sign * d, 8)], index, axis=1, mode="promise_in_bounds")
                        for d in range(REACH + 1)
                    ]
                    total[j] = total[j] + g * jnp.where(near, pick[0], jnp.where(next_, pick[1], pick[2]))
            for j in names:
                new[j, pl.ds(to, 8)] = total[j]

        low, high = (0, 1), tuple(range(2, 9))
        buffers = (even, odd)
        def relax(harmonics, sweeps):
            for s in range(sweeps):
                wide = (sweeps - 1 - s) * REACH
                old, new = buffers[s % 2], buffers[(s + 1) % 2]
                for start in tiles(RIM - wide, RIM + OWN + wide):
                    if s < sweeps - 1:
                        sweep(old, new, start, start, harmonics)
                    else:
                        sweep(old, fin, start, start - RIM, harmonics)

        relax(high, SWEEPS_FINE)

        @pl.when(has_outer)
        def _():
            all_of(rf, r_far)

        transform(far(rf, 0), FAR, even, at_outer[1], forward_low)
        transform(far(rf, 1), FAR_S, src, at_outer[2], forward_low)
        relax(low, SWEEPS)
        for t in range(0, OWN, 8):
            rows = pl.ds(t, 8)
            x = backward([fin[j, rows] for j in range(NI)])
            for n in range(NI):
                back[n // PER, n % PER, rows] = x[n]
        home = [remote(back.at[i], out.at[:, mine], s_out, r_out, cell, i) for i in range(GROUP)]
        for i in range(GROUP):

            @pl.when(inst != i)
            def _():
                home[i].start()

        out[:, mine] = back[inst]
        all_of(back.at[pl.ds(1, GROUP - 1)], s_out)

        all_of(sx.at[pl.ds(1, COMP - 1)], s_own)
        stat_flip.wait_send()
        rim_flip.wait_send()
        all_of(out.at[:, pl.ds(1, COMP - 1)], r_out)

    @pl.when(idle)
    def _():
        pltpu.make_async_copy(sx, sx, s_own).wait()
        pltpu.make_async_copy(out, out, r_out).wait()

    @pl.when(give)
    def _():
        stat_outer.wait_send()

    @pl.when(has_outer)
    def _():
        pltpu.make_async_copy(sn, sn, s_near).wait()
        pltpu.make_async_copy(sf, sf, s_far).wait()


def per_device(initial, source, neighbors, face_weights, damping):
    vmem = pl.BlockSpec(memory_space=pltpu.VMEM)
    f32, i32 = jnp.float32, jnp.int32
    dma = pltpu.SemaphoreType.DMA
    arguments = (initial, source, neighbors, face_weights, damping.reshape(OWN, LANES))
    result = pl.pallas_call(
        kernel,
        out_shape=pltpu.VMEM((PER, COMP, OWN, LANES), f32),
        in_specs=[pl.BlockSpec(memory_space=pltpu.HBM)] * 5,
        out_specs=vmem,
        scratch_shapes=[
            pltpu.VMEM((PER * COMP, OWN * LANES), f32),
            pltpu.VMEM((PER * COMP, OWN * LANES), f32),
            pltpu.VMEM((NEIGH, OWN * LANES), i32),
            pltpu.VMEM((NEIGH, OWN * LANES), f32),
            pltpu.VMEM((OWN, LANES), f32),
            pltpu.VMEM((COMP, 2, PER, OWN, LANES), f32),
            pltpu.VMEM((COMP, M_NEAR, LANES), f32),
            pltpu.VMEM((COMP, M_FAR, LANES), f32),
            pltpu.VMEM((2 * NEIGH + 1, RIM_S, LANES), f32),
            pltpu.VMEM((2 * NEIGH + 1, RIM_S, LANES), f32),
            pltpu.VMEM((GROUP, 2, PER, OWN, LANES), f32),
            pltpu.VMEM((GROUP, M_NEAR, LANES), f32),
            pltpu.VMEM((GROUP, M_FAR, LANES), f32),
            pltpu.VMEM((2 * NEIGH + 1, RIM_S, LANES), f32),
            pltpu.VMEM((2 * NEIGH + 1, RIM_S, LANES), f32),
            pltpu.VMEM((NI + 2 * LOW, 8, LANES), f32),
            pltpu.VMEM((NI + 2 * LOW, 8, LANES), f32),
            pltpu.VMEM((NEIGH, ROWS, LANES), i32),
            pltpu.VMEM((NEIGH, ROWS, LANES), i32),
            pltpu.VMEM((NEIGH, ROWS, LANES), f32),
            pltpu.VMEM((ROWS, LANES), f32),
            pltpu.VMEM((NI, ROWS, LANES), f32),
            pltpu.VMEM((NI, ROWS, LANES), f32),
            pltpu.VMEM((NI, ROWS, LANES), f32),
            pltpu.VMEM((NI, OWN, LANES), f32),
            pltpu.VMEM((GROUP, PER, OWN, LANES), f32),
            dma((5,)), dma, dma, dma, dma((2,)), dma, dma, dma, dma, dma((2,)), dma, dma, dma,
        ],
        compiler_params=pltpu.CompilerParams(
            collective_id=0, has_side_effects=True, vmem_limit_bytes=32 * 1024 * 1024
        ),
    )(*(pltpu.with_memory_space_constraint(x, pltpu.HBM) for x in arguments))
    return result.reshape(PER * COMP, OWN * LANES)


def solution(mesh):
    return jax.shard_map(
        per_device,
        mesh=mesh,
        in_specs=(
            P("inst", "cell"),
            P("inst", "cell"),
            P(None, "cell"),
            P(None, "cell"),
            P("cell"),
        ),
        out_specs=P("inst", "cell"),
        check_vma=False,
    )
```

```python
import math

import jax
import jax.numpy as jnp
from jax import lax
from jax.experimental import pallas as pl
from jax.experimental.pallas import tpu as pltpu
from jax.sharding import PartitionSpec as P

NI = 16
COMP = 5
NEIGH = 4
FREQ = 0.15
RELAX = 0.6
LANES = 128
OWN = 16
SWEEPS_FINE = 2
SWEEPS = 5
REACH = 2
RIM = SWEEPS * REACH
RIM_S = RIM - REACH
ROWS = OWN + 2 * RIM
GROUP = 8
PER = NI // GROUP
NEAR = SWEEPS_FINE * REACH
FAR, FAR_S = RIM - NEAR, RIM_S - NEAR
LOW = 3
M_NEAR, M_FAR = 16, PER * (FAR + FAR_S)
OWNERS = ((1, 2, 3, 4, 6), (0, 1, 2, 4, 6))
MESH = pl.DeviceIdType.MESH
ROOT = math.sqrt(0.5)


def forward(x):
    out = [None] * NI
    p = [x[n] + x[n + 8] for n in range(8)]
    q = [x[n] - x[n + 8] for n in range(8)]
    q0, q4 = q[0] * 0.125, q[4] * 0.125
    d = [None] + [q[n] - q[8 - n] for n in (1, 2, 3)]
    s = [None] + [q[n] + q[8 - n] for n in (1, 2, 3)]
    for k in (1, 3, 5, 7):
        a, b = q0, (q4 if k in (1, 5) else -q4)
        for n in (1, 2, 3):
            a = a + d[n] * (math.cos(math.pi * k * n / 8) / 8)
            b = b + s[n] * (math.sin(math.pi * k * n / 8) / 8)
        out[2 * k - 1], out[2 * k] = a, b
    pp = [p[n] + p[n + 4] for n in range(4)]
    pq = [p[n] - p[n + 4] for n in range(4)]
    a, b = pq[0] * 0.125, pq[2] * 0.125
    d1, s1 = (pq[1] - pq[3]) * (ROOT / 8), (pq[1] + pq[3]) * (ROOT / 8)
    out[3], out[4] = a + d1, s1 + b
    out[11], out[12] = a - d1, s1 - b
    out[7], out[8] = (pp[0] - pp[2]) * 0.125, (pp[1] - pp[3]) * 0.125
    even, odd = (pp[0] + pp[2]) * 0.0625, (pp[1] + pp[3]) * 0.0625
    out[0], out[15] = even + odd, even - odd
    return out


def forward_low(x):
    p = [x[n] + x[n + 8] for n in range(8)]
    q = [x[n] - x[n + 8] for n in range(8)]
    a, b = q[0] * 0.125, q[4] * 0.125
    for n in (1, 2, 3):
        a = a + (q[n] - q[8 - n]) * (math.cos(math.pi * n / 8) / 8)
        b = b + (q[n] + q[8 - n]) * (math.sin(math.pi * n / 8) / 8)
    return [(((p[0] + p[4]) + (p[2] + p[6])) + ((p[1] + p[5]) + (p[3] + p[7]))) * 0.0625, a, b]


def backward(h):
    a = {k: h[2 * k - 1] for k in range(1, 9)}
    a[0] = h[0]
    b = {k: h[2 * k] for k in range(1, 8)}
    odd = [None] * 8
    odd[0] = (a[1] + a[3]) + (a[5] + a[7])
    odd[4] = (b[1] - b[3]) + (b[5] - b[7])
    for n in (1, 2, 3):
        c = s = 0.0
        for k in (1, 3, 5, 7):
            c = c + a[k] * math.cos(math.pi * k * n / 8)
            s = s + b[k] * math.sin(math.pi * k * n / 8)
        odd[n], odd[8 - n] = s + c, s - c
    d, s = (a[2] - a[6]) * ROOT, (b[2] + b[6]) * ROOT
    half = [a[2] + a[6], s + d, b[2] - b[6], s - d]
    up, down = a[0] + a[8], a[0] - a[8]
    quarter = [up + a[4], down + b[4], up - a[4], down - b[4]]
    even = [quarter[n] + half[n] for n in range(4)] + [quarter[n] - half[n] for n in range(4)]
    return [even[n] + odd[n] for n in range(8)] + [even[n] - odd[n] for n in range(8)]


def tiles(start, stop):
    return [min(row, stop - 8) for row in range(start, stop, 8)]


def kernel(
    initial_in, source_in, neighbors_in, weights_in, damping_in, out,
    initial, source, neighbors, weights, damping,
    sx, sn, sf, st_outer, st_flip, ro, rn, rf, got_outer, got_flip, hs, hr,
    lane, step, gain, scale, even, odd, src, fin, back,
    s_in, s_own, s_near, s_far, s_stat, s_rim, r_own, r_near, r_far, r_stat, r_rim, s_out, r_out,
):
    cell, inst = lax.axis_index("cell"), lax.axis_index("inst")
    count = lax.axis_size("cell")
    odd_block = lax.rem(cell, 2)
    is_even = odd_block == 0
    flip = cell + 1 - 2 * odd_block
    beyond = cell - 1 + 2 * odd_block
    has_outer = jnp.logical_and(beyond >= 0, beyond < count)
    outer = jnp.minimum(jnp.maximum(beyond, 0), count - 1)

    def owners(c):
        high = lax.rem(lax.div(c, 2), 2)
        return [OWNERS[0][v] + high * (OWNERS[1][v] - OWNERS[0][v]) for v in range(COMP)]

    here, there = owners(cell), owners(cell + 2)
    mine, owns, serves = 0, 0, 0
    for v in range(COMP):
        hit = (inst == here[v]).astype(jnp.int32)
        mine, owns = mine + v * hit, owns + hit
        serves = serves + (inst == there[v]).astype(jnp.int32)
    busy = owns == 1
    idle = jnp.logical_not(busy)
    give = jnp.logical_and(has_outer, serves == 1)

    load = [
        pltpu.make_async_copy(a, b, s_in.at[j])
        for j, (a, b) in enumerate(
            (
                (initial_in, initial),
                (source_in, source),
                (neighbors_in, neighbors),
                (weights_in, weights),
                (damping_in, damping),
            )
        )
    ]
    for copy in load:
        copy.start()

    barrier = pltpu.get_barrier_semaphore()

    def greet(c, i):
        pl.semaphore_signal(barrier, inc=1, device_id={"cell": c, "inst": i}, device_id_type=MESH)

    @pl.when(busy)
    def _():
        @pl.when(has_outer)
        def _():
            for i in range(GROUP):
                greet(outer, i)

        greet(flip, inst)
        for j in range(1, GROUP):
            greet(cell, lax.rem(inst + j, GROUP))

    for copy in load[2:]:
        copy.wait()
    w = [weights[pl.ds(k, 1), :].reshape(OWN, LANES) for k in range(NEIGH)]
    off = [neighbors[pl.ds(k, 1), :].reshape(OWN, LANES) for k in range(NEIGH)]
    m = RELAX / (damping[...] + ((w[0] + w[1]) + (w[2] + w[3])))
    own = pl.ds(RIM, OWN)
    scale[own] = m

    def edges(k, x):
        head, tail = x[:RIM_S], x[OWN - RIM_S :]
        st_outer[k], st_flip[k] = jnp.where(is_even, head, tail), jnp.where(is_even, tail, head)

    edges(2 * NEIGH, m)
    for k in range(NEIGH):
        g = w[k] * m
        position = lax.broadcasted_iota(jnp.int32, (OWN, LANES), 1) + off[k]
        lane[k, own] = position & (LANES - 1)
        step[k, own] = position >> 7
        gain[k, own] = g
        edges(k, off[k].astype(jnp.float32))
        edges(NEIGH + k, g)

    hs[NI:] = jnp.zeros((2 * LOW, 8, LANES), jnp.float32)

    for which, ref in enumerate((initial, source)):
        load[which].wait()
        for n in range(PER):
            for v in range(COMP):
                x = ref[pl.ds(n * COMP + v, 1), :].reshape(OWN, LANES)
                sx[v, which, n] = x
                near_rows = pl.ds((which * PER + n) * NEAR, NEAR)
                sn[v, near_rows] = jnp.where(is_even, x[:NEAR], x[OWN - NEAR :])
                size = (FAR, FAR_S)[which]
                far_rows = pl.ds((n * FAR, PER * FAR + n * FAR_S)[which], size)
                sf[v, far_rows] = jnp.where(is_even, x[NEAR : NEAR + size], x[OWN - NEAR - size : OWN - NEAR])

    pl.semaphore_wait(barrier, COMP * (1 + has_outer.astype(jnp.int32)))

    def remote(a, b, s, r, c, i):
        return pltpu.make_async_remote_copy(
            src_ref=a, dst_ref=b, send_sem=s, recv_sem=r, device_id={"cell": c, "inst": i}, device_id_type=MESH
        )

    own_copy = [remote(sx.at[v], ro.at[inst], s_own, r_own, cell, here[v]) for v in range(COMP)]
    near_copy = [remote(sn.at[v], rn.at[inst], s_near, r_near, outer, there[v]) for v in range(COMP)]
    far_copy = [remote(sf.at[v], rf.at[inst], s_far, r_far, outer, there[v]) for v in range(COMP)]
    stat_outer = remote(st_outer, got_outer, s_stat.at[0], r_stat.at[0], outer, inst)
    stat_flip = remote(st_flip, got_flip, s_stat.at[1], r_stat.at[1], flip, inst)
    rim_flip = remote(hs, hr, s_rim, r_rim, flip, inst)

    for v in range(COMP):

        @pl.when(mine + COMP * (1 - owns) != v)
        def _():
            own_copy[v].start()

    @pl.when(has_outer)
    def _():
        for v in range(COMP):
            near_copy[v].start()

    @pl.when(give)
    def _():
        stat_outer.start()

    @pl.when(has_outer)
    def _():
        for v in range(COMP):
            far_copy[v].start()

    @pl.when(busy)
    def _():
        stat_flip.start()
        ro[inst] = sx[mine]

        @pl.when(has_outer)
        def _():
            stat_outer.wait_recv()

        @pl.when(jnp.logical_not(has_outer))
        def _():
            rn[...] = jnp.zeros_like(rn)
            rf[...] = jnp.zeros_like(rf)
            got_outer[...] = jnp.zeros_like(got_outer)

        stat_flip.wait_recv()

        def pick(even_row, odd_row):
            return even_row + odd_block * (odd_row - even_row)

        left, right = (RIM - NEAR, 0, FAR - FAR_S), (RIM + OWN, RIM + OWN + NEAR, RIM + OWN + NEAR)
        at_outer = [pick(a, b) for a, b in zip(left, right)]
        at_flip = [pick(b, a) for a, b in zip(left, right)]
        for start, got in (
            (pick(RIM - RIM_S, RIM + OWN), got_outer),
            (pick(RIM + OWN, RIM - RIM_S), got_flip),
        ):
            rows = pl.ds(start, RIM_S)
            for k in range(NEIGH):
                position = lax.broadcasted_iota(jnp.int32, (RIM_S, LANES), 1) + got[k].astype(jnp.int32)
                lane[k, rows] = position & (LANES - 1)
                step[k, rows] = position >> 7
                gain[k, rows] = got[NEIGH + k]
            scale[rows] = got[2 * NEIGH]

        def transform(read, rows, dst, to, change=forward):
            h = change([read(n) for n in range(NI)])
            for j in range(len(h)):
                dst[j, pl.ds(to, rows)] = h[j]

        def near(ref, which):
            return lambda n: ref[n // PER, pl.ds((which * PER + n % PER) * NEAR, NEAR)]

        def far(ref, which):
            base, size = (0, PER * FAR)[which], (FAR, FAR_S)[which]
            return lambda n: ref[n // PER, pl.ds(base + (n % PER) * size, size)]

        def all_of(ref, sem):
            pltpu.make_async_copy(ref, ref, sem).wait()

        def sweep(old, new, start, to, harmonics):
            rows = pl.ds(start, 8)
            m = scale[rows]
            names = [j for k in harmonics for j in ((2 * k - 1, 2 * k) if 0 < k < 8 else (max(2 * k - 1, 0),))]
            total = {}
            for k in harmonics:
                if k in (0, 8):
                    j = max(2 * k - 1, 0)
                    total[j] = (1.0 - RELAX) * old[j, rows] + m * src[j, rows]
                else:
                    a, b = 2 * k - 1, 2 * k
                    xa, xb = old[a, rows], old[b, rows]
                    total[a] = (1.0 - RELAX) * xa + m * (src[a, rows] - (FREQ * k) * xb)
                    total[b] = (1.0 - RELAX) * xb + m * (src[b, rows] + (FREQ * k) * xa)
            for k in range(NEIGH):
                sign = 1 if k % 2 else -1
                index, by, g = lane[k, rows], step[k, rows], gain[k, rows]
                near, next_ = by == 0, by == sign
                for j in names:
                    pick = [
                        jnp.take_along_axis(old[j, pl.ds(start + sign * d, 8)], index, axis=1, mode="promise_in_bounds")
                        for d in range(REACH + 1)
                    ]
                    total[j] = total[j] + g * jnp.where(near, pick[0], jnp.where(next_, pick[1], pick[2]))
            for j in names:
                new[j, pl.ds(to, 8)] = total[j]

        low, high = (0, 1), tuple(range(2, 9))
        buffers = (even, odd)
        def relax(harmonics, sweeps, first=0):
            for s in range(first, sweeps):
                wide = (sweeps - 1 - s) * REACH
                old, new = buffers[s % 2], buffers[(s + 1) % 2]
                for start in tiles(RIM - wide, RIM + OWN + wide):
                    if s < sweeps - 1:
                        sweep(old, new, start, start, harmonics)
                    else:
                        sweep(old, fin, start, start - RIM, harmonics)

        all_of(ro.at[pl.ds(1, GROUP - 1)], r_own)
        for t in range(0, OWN, 8):
            for which, dst in ((0, even), (1, src)):
                transform(lambda n: ro[n // PER, which, n % PER, pl.ds(t, 8)], 8, dst, RIM + t)

        to_near, to_far, to_far_s = pick(RIM + OWN - NEAR, RIM), pick(RIM + OWN - RIM, RIM + NEAR), pick(RIM + OWN - RIM_S, RIM + NEAR)
        for j in range(NI):
            hs[j, :NEAR], hs[j, NEAR:] = even[j, pl.ds(to_near, NEAR)], src[j, pl.ds(to_near, NEAR)]
        for j in range(LOW):
            hs[NI + j, :FAR] = even[j, pl.ds(to_far, FAR)]
            hs[NI + LOW + j, :FAR_S] = src[j, pl.ds(to_far_s, FAR_S)]
        rim_flip.start()
        ends = (RIM - REACH, RIM + OWN + REACH - 8)
        sweep(even, odd, RIM + 6, RIM + 6, high)

        @pl.when(has_outer)
        def _():
            all_of(rn, r_near)

        for which, dst in ((0, even), (1, src)):
            transform(near(rn, which), NEAR, dst, at_outer[0])
        start = pick(*ends)
        sweep(even, odd, start, start, high)
        rim_flip.wait_recv()
        for j in range(NI):
            even[j, pl.ds(at_flip[0], NEAR)], src[j, pl.ds(at_flip[0], NEAR)] = hr[j, :NEAR], hr[j, NEAR:]
        for j in range(LOW):
            even[j, pl.ds(at_flip[1], FAR)] = hr[NI + j, :FAR]
            src[j, pl.ds(at_flip[2], FAR_S)] = hr[NI + LOW + j, :FAR_S]

        start = pick(*ends[::-1])
        sweep(even, odd, start, start, high)
        relax(high, SWEEPS_FINE, 1)

        @pl.when(has_outer)
        def _():
            all_of(rf, r_far)

        transform(far(rf, 0), FAR, even, at_outer[1], forward_low)
        transform(far(rf, 1), FAR_S, src, at_outer[2], forward_low)
        relax(low, SWEEPS)
        for t in range(0, OWN, 8):
            rows = pl.ds(t, 8)
            x = backward([fin[j, rows] for j in range(NI)])
            for n in range(NI):
                back[n // PER, n % PER, rows] = x[n]
        home = [remote(back.at[i], out.at[:, mine], s_out, r_out, cell, i) for i in range(GROUP)]
        for i in range(GROUP):

            @pl.when(inst != i)
            def _():
                home[i].start()

        out[:, mine] = back[inst]
        all_of(back.at[pl.ds(1, GROUP - 1)], s_out)

        all_of(sx.at[pl.ds(1, COMP - 1)], s_own)
        stat_flip.wait_send()
        rim_flip.wait_send()
        all_of(out.at[:, pl.ds(1, COMP - 1)], r_out)

    @pl.when(idle)
    def _():
        pltpu.make_async_copy(sx, sx, s_own).wait()
        pltpu.make_async_copy(out, out, r_out).wait()

    @pl.when(give)
    def _():
        stat_outer.wait_send()

    @pl.when(has_outer)
    def _():
        pltpu.make_async_copy(sn, sn, s_near).wait()
        pltpu.make_async_copy(sf, sf, s_far).wait()


def per_device(initial, source, neighbors, face_weights, damping):
    vmem = pl.BlockSpec(memory_space=pltpu.VMEM)
    f32, i32 = jnp.float32, jnp.int32
    dma = pltpu.SemaphoreType.DMA
    arguments = (initial, source, neighbors, face_weights, damping.reshape(OWN, LANES))
    result = pl.pallas_call(
        kernel,
        out_shape=pltpu.VMEM((PER, COMP, OWN, LANES), f32),
        in_specs=[pl.BlockSpec(memory_space=pltpu.HBM)] * 5,
        out_specs=vmem,
        scratch_shapes=[
            pltpu.VMEM((PER * COMP, OWN * LANES), f32),
            pltpu.VMEM((PER * COMP, OWN * LANES), f32),
            pltpu.VMEM((NEIGH, OWN * LANES), i32),
            pltpu.VMEM((NEIGH, OWN * LANES), f32),
            pltpu.VMEM((OWN, LANES), f32),
            pltpu.VMEM((COMP, 2, PER, OWN, LANES), f32),
            pltpu.VMEM((COMP, M_NEAR, LANES), f32),
            pltpu.VMEM((COMP, M_FAR, LANES), f32),
            pltpu.VMEM((2 * NEIGH + 1, RIM_S, LANES), f32),
            pltpu.VMEM((2 * NEIGH + 1, RIM_S, LANES), f32),
            pltpu.VMEM((GROUP, 2, PER, OWN, LANES), f32),
            pltpu.VMEM((GROUP, M_NEAR, LANES), f32),
            pltpu.VMEM((GROUP, M_FAR, LANES), f32),
            pltpu.VMEM((2 * NEIGH + 1, RIM_S, LANES), f32),
            pltpu.VMEM((2 * NEIGH + 1, RIM_S, LANES), f32),
            pltpu.VMEM((NI + 2 * LOW, 8, LANES), f32),
            pltpu.VMEM((NI + 2 * LOW, 8, LANES), f32),
            pltpu.VMEM((NEIGH, ROWS, LANES), i32),
            pltpu.VMEM((NEIGH, ROWS, LANES), i32),
            pltpu.VMEM((NEIGH, ROWS, LANES), f32),
            pltpu.VMEM((ROWS, LANES), f32),
            pltpu.VMEM((NI, ROWS, LANES), f32),
            pltpu.VMEM((NI, ROWS, LANES), f32),
            pltpu.VMEM((NI, ROWS, LANES), f32),
            pltpu.VMEM((NI, OWN, LANES), f32),
            pltpu.VMEM((GROUP, PER, OWN, LANES), f32),
            dma((5,)), dma, dma, dma, dma((2,)), dma, dma, dma, dma, dma((2,)), dma, dma, dma,
        ],
        compiler_params=pltpu.CompilerParams(
            collective_id=0, has_side_effects=True, vmem_limit_bytes=32 * 1024 * 1024
        ),
    )(*(pltpu.with_memory_space_constraint(x, pltpu.HBM) for x in arguments))
    return result.reshape(PER * COMP, OWN * LANES)


def solution(mesh):
    return jax.shard_map(
        per_device,
        mesh=mesh,
        in_specs=(
            P("inst", "cell"),
            P("inst", "cell"),
            P(None, "cell"),
            P(None, "cell"),
            P("cell"),
        ),
        out_specs=P("inst", "cell"),
        check_vma=False,
    )
```

```python
import math

import jax
import jax.numpy as jnp
from jax import lax
from jax.experimental import pallas as pl
from jax.experimental.pallas import tpu as pltpu
from jax.sharding import PartitionSpec as P

NI = 16
COMP = 5
NEIGH = 4
FREQ = 0.15
RELAX = 0.6
LANES = 128
OWN = 16
SWEEPS_FINE = 2
SWEEPS = 5
REACH = 2
RIM = SWEEPS * REACH
RIM_S = RIM - REACH
ROWS = OWN + 2 * RIM
GROUP = 8
PER = NI // GROUP
NEAR = SWEEPS_FINE * REACH
FAR, FAR_S = RIM - NEAR, RIM_S - NEAR
LOW = 3
M_NEAR, M_FAR = 16, PER * (FAR + FAR_S)
OWNERS = ((1, 2, 3, 4, 6), (0, 1, 2, 4, 6))
MESH = pl.DeviceIdType.MESH
ROOT = math.sqrt(0.5)


def forward(x):
    out = [None] * NI
    p = [x[n] + x[n + 8] for n in range(8)]
    q = [x[n] - x[n + 8] for n in range(8)]
    q0, q4 = q[0] * 0.125, q[4] * 0.125
    d = [None] + [q[n] - q[8 - n] for n in (1, 2, 3)]
    s = [None] + [q[n] + q[8 - n] for n in (1, 2, 3)]
    for k in (1, 3, 5, 7):
        a, b = q0, (q4 if k in (1, 5) else -q4)
        for n in (1, 2, 3):
            a = a + d[n] * (math.cos(math.pi * k * n / 8) / 8)
            b = b + s[n] * (math.sin(math.pi * k * n / 8) / 8)
        out[2 * k - 1], out[2 * k] = a, b
    pp = [p[n] + p[n + 4] for n in range(4)]
    pq = [p[n] - p[n + 4] for n in range(4)]
    a, b = pq[0] * 0.125, pq[2] * 0.125
    d1, s1 = (pq[1] - pq[3]) * (ROOT / 8), (pq[1] + pq[3]) * (ROOT / 8)
    out[3], out[4] = a + d1, s1 + b
    out[11], out[12] = a - d1, s1 - b
    out[7], out[8] = (pp[0] - pp[2]) * 0.125, (pp[1] - pp[3]) * 0.125
    even, odd = (pp[0] + pp[2]) * 0.0625, (pp[1] + pp[3]) * 0.0625
    out[0], out[15] = even + odd, even - odd
    return out


def forward_low(x):
    p = [x[n] + x[n + 8] for n in range(8)]
    q = [x[n] - x[n + 8] for n in range(8)]
    a, b = q[0] * 0.125, q[4] * 0.125
    for n in (1, 2, 3):
        a = a + (q[n] - q[8 - n]) * (math.cos(math.pi * n / 8) / 8)
        b = b + (q[n] + q[8 - n]) * (math.sin(math.pi * n / 8) / 8)
    return [(((p[0] + p[4]) + (p[2] + p[6])) + ((p[1] + p[5]) + (p[3] + p[7]))) * 0.0625, a, b]


def backward(h):
    a = {k: h[2 * k - 1] for k in range(1, 9)}
    a[0] = h[0]
    b = {k: h[2 * k] for k in range(1, 8)}
    odd = [None] * 8
    odd[0] = (a[1] + a[3]) + (a[5] + a[7])
    odd[4] = (b[1] - b[3]) + (b[5] - b[7])
    for n in (1, 2, 3):
        c = s = 0.0
        for k in (1, 3, 5, 7):
            c = c + a[k] * math.cos(math.pi * k * n / 8)
            s = s + b[k] * math.sin(math.pi * k * n / 8)
        odd[n], odd[8 - n] = s + c, s - c
    d, s = (a[2] - a[6]) * ROOT, (b[2] + b[6]) * ROOT
    half = [a[2] + a[6], s + d, b[2] - b[6], s - d]
    up, down = a[0] + a[8], a[0] - a[8]
    quarter = [up + a[4], down + b[4], up - a[4], down - b[4]]
    even = [quarter[n] + half[n] for n in range(4)] + [quarter[n] - half[n] for n in range(4)]
    return [even[n] + odd[n] for n in range(8)] + [even[n] - odd[n] for n in range(8)]


def tiles(start, stop):
    return [min(row, stop - 8) for row in range(start, stop, 8)]


def kernel(
    initial_in, source_in, neighbors_in, weights_in, damping_in, out,
    initial, source, neighbors, weights, damping,
    sx, sn, sf, st_outer, st_flip, ro, rn, rf, got_outer, got_flip, hs, hr,
    lane, step, gain, scale, even, odd, src, fin, back,
    s_in, s_own, s_near, s_far, s_stat, s_rim, r_own, r_near, r_far, r_stat, r_rim, s_out, r_out,
):
    cell, inst = lax.axis_index("cell"), lax.axis_index("inst")
    count = lax.axis_size("cell")
    odd_block = lax.rem(cell, 2)
    is_even = odd_block == 0
    flip = cell + 1 - 2 * odd_block
    beyond = cell - 1 + 2 * odd_block
    has_outer = jnp.logical_and(beyond >= 0, beyond < count)
    outer = jnp.minimum(jnp.maximum(beyond, 0), count - 1)

    def owners(c):
        high = lax.rem(lax.div(c, 2), 2)
        return [OWNERS[0][v] + high * (OWNERS[1][v] - OWNERS[0][v]) for v in range(COMP)]

    here, there = owners(cell), owners(cell + 2)
    mine, owns, serves = 0, 0, 0
    for v in range(COMP):
        hit = (inst == here[v]).astype(jnp.int32)
        mine, owns = mine + v * hit, owns + hit
        serves = serves + (inst == there[v]).astype(jnp.int32)
    busy = owns == 1
    idle = jnp.logical_not(busy)
    give = jnp.logical_and(has_outer, serves == 1)

    barrier = pltpu.get_barrier_semaphore()

    def greet(c, i):
        pl.semaphore_signal(barrier, inc=1, device_id={"cell": c, "inst": i}, device_id_type=MESH)

    @pl.when(busy)
    def _():
        for j in range(1, GROUP):
            greet(cell, lax.rem(inst + j, GROUP))

    load = [
        pltpu.make_async_copy(a, b, s_in.at[j])
        for j, (a, b) in enumerate(
            (
                (initial_in, initial),
                (source_in, source),
                (neighbors_in, neighbors),
                (weights_in, weights),
                (damping_in, damping),
            )
        )
    ]
    for copy in load:
        copy.start()

    @pl.when(busy)
    def _():
        @pl.when(has_outer)
        def _():
            for i in range(GROUP):
                greet(outer, i)

        greet(flip, inst)

    for copy in load[2:]:
        copy.wait()
    w = [weights[pl.ds(k, 1), :].reshape(OWN, LANES) for k in range(NEIGH)]
    off = [neighbors[pl.ds(k, 1), :].reshape(OWN, LANES) for k in range(NEIGH)]
    m = RELAX / (damping[...] + ((w[0] + w[1]) + (w[2] + w[3])))
    own = pl.ds(RIM, OWN)
    scale[own] = m

    def edges(k, x):
        head, tail = x[:RIM_S], x[OWN - RIM_S :]
        st_outer[k], st_flip[k] = jnp.where(is_even, head, tail), jnp.where(is_even, tail, head)

    edges(2 * NEIGH, m)
    for k in range(NEIGH):
        g = w[k] * m
        position = lax.broadcasted_iota(jnp.int32, (OWN, LANES), 1) + off[k]
        lane[k, own] = position & (LANES - 1)
        step[k, own] = position >> 7
        gain[k, own] = g
        edges(k, off[k].astype(jnp.float32))
        edges(NEIGH + k, g)

    hs[NI:] = jnp.zeros((2 * LOW, 8, LANES), jnp.float32)

    for which, ref in enumerate((initial, source)):
        load[which].wait()
        for n in range(PER):
            for v in range(COMP):
                x = ref[pl.ds(n * COMP + v, 1), :].reshape(OWN, LANES)
                sx[v, which, n] = x
                near_rows = pl.ds((which * PER + n) * NEAR, NEAR)
                sn[v, near_rows] = jnp.where(is_even, x[:NEAR], x[OWN - NEAR :])
                size = (FAR, FAR_S)[which]
                far_rows = pl.ds((n * FAR, PER * FAR + n * FAR_S)[which], size)
                sf[v, far_rows] = jnp.where(is_even, x[NEAR : NEAR + size], x[OWN - NEAR - size : OWN - NEAR])

    pl.semaphore_wait(barrier, COMP * (1 + has_outer.astype(jnp.int32)))

    def remote(a, b, s, r, c, i):
        return pltpu.make_async_remote_copy(
            src_ref=a, dst_ref=b, send_sem=s, recv_sem=r, device_id={"cell": c, "inst": i}, device_id_type=MESH
        )

    own_copy = [remote(sx.at[v], ro.at[inst], s_own, r_own, cell, here[v]) for v in range(COMP)]
    near_copy = [remote(sn.at[v], rn.at[inst], s_near, r_near, outer, there[v]) for v in range(COMP)]
    far_copy = [remote(sf.at[v], rf.at[inst], s_far, r_far, outer, there[v]) for v in range(COMP)]
    stat_outer = remote(st_outer, got_outer, s_stat.at[0], r_stat.at[0], outer, inst)
    stat_flip = remote(st_flip, got_flip, s_stat.at[1], r_stat.at[1], flip, inst)
    rim_flip = remote(hs, hr, s_rim, r_rim, flip, inst)

    for v in range(COMP):

        @pl.when(mine + COMP * (1 - owns) != v)
        def _():
            own_copy[v].start()

    @pl.when(has_outer)
    def _():
        for v in range(COMP):
            near_copy[v].start()

    @pl.when(give)
    def _():
        stat_outer.start()

    @pl.when(has_outer)
    def _():
        for v in range(COMP):
            far_copy[v].start()

    @pl.when(busy)
    def _():
        stat_flip.start()
        ro[inst] = sx[mine]

        @pl.when(has_outer)
        def _():
            stat_outer.wait_recv()

        @pl.when(jnp.logical_not(has_outer))
        def _():
            rn[...] = jnp.zeros_like(rn)
            rf[...] = jnp.zeros_like(rf)
            got_outer[...] = jnp.zeros_like(got_outer)

        stat_flip.wait_recv()

        def pick(even_row, odd_row):
            return even_row + odd_block * (odd_row - even_row)

        left, right = (RIM - NEAR, 0, FAR - FAR_S), (RIM + OWN, RIM + OWN + NEAR, RIM + OWN + NEAR)
        at_outer = [pick(a, b) for a, b in zip(left, right)]
        at_flip = [pick(b, a) for a, b in zip(left, right)]
        for start, got in (
            (pick(RIM - RIM_S, RIM + OWN), got_outer),
            (pick(RIM + OWN, RIM - RIM_S), got_flip),
        ):
            rows = pl.ds(start, RIM_S)
            for k in range(NEIGH):
                position = lax.broadcasted_iota(jnp.int32, (RIM_S, LANES), 1) + got[k].astype(jnp.int32)
                lane[k, rows] = position & (LANES - 1)
                step[k, rows] = position >> 7
                gain[k, rows] = got[NEIGH + k]
            scale[rows] = got[2 * NEIGH]

        def transform(read, rows, dst, to, change=forward):
            h = change([read(n) for n in range(NI)])
            for j in range(len(h)):
                dst[j, pl.ds(to, rows)] = h[j]

        def near(ref, which):
            return lambda n: ref[n // PER, pl.ds((which * PER + n % PER) * NEAR, NEAR)]

        def far(ref, which):
            base, size = (0, PER * FAR)[which], (FAR, FAR_S)[which]
            return lambda n: ref[n // PER, pl.ds(base + (n % PER) * size, size)]

        def all_of(ref, sem):
            pltpu.make_async_copy(ref, ref, sem).wait()

        def sweep(old, new, start, to, harmonics):
            rows = pl.ds(start, 8)
            m = scale[rows]
            names = [j for k in harmonics for j in ((2 * k - 1, 2 * k) if 0 < k < 8 else (max(2 * k - 1, 0),))]
            total = {}
            for k in harmonics:
                if k in (0, 8):
                    j = max(2 * k - 1, 0)
                    total[j] = (1.0 - RELAX) * old[j, rows] + m * src[j, rows]
                else:
                    a, b = 2 * k - 1, 2 * k
                    xa, xb = old[a, rows], old[b, rows]
                    total[a] = (1.0 - RELAX) * xa + m * (src[a, rows] - (FREQ * k) * xb)
                    total[b] = (1.0 - RELAX) * xb + m * (src[b, rows] + (FREQ * k) * xa)
            for k in range(NEIGH):
                sign = 1 if k % 2 else -1
                index, by, g = lane[k, rows], step[k, rows], gain[k, rows]
                near, next_ = by == 0, by == sign
                for j in names:
                    pick = [
                        jnp.take_along_axis(old[j, pl.ds(start + sign * d, 8)], index, axis=1, mode="promise_in_bounds")
                        for d in range(REACH + 1)
                    ]
                    total[j] = total[j] + g * jnp.where(near, pick[0], jnp.where(next_, pick[1], pick[2]))
            for j in names:
                new[j, pl.ds(to, 8)] = total[j]

        low, high = (0, 1), tuple(range(2, 9))
        buffers = (even, odd)
        def relax(harmonics, sweeps, s):
            wide = (sweeps - 1 - s) * REACH
            old, new = buffers[s % 2], buffers[(s + 1) % 2]
            for start in tiles(RIM - wide, RIM + OWN + wide):
                if s < sweeps - 1:
                    sweep(old, new, start, start, harmonics)
                else:
                    sweep(old, fin, start, start - RIM, harmonics)

        all_of(ro.at[pl.ds(1, GROUP - 1)], r_own)
        for t in range(0, OWN, 8):
            for which, dst in ((0, even), (1, src)):
                transform(lambda n: ro[n // PER, which, n % PER, pl.ds(t, 8)], 8, dst, RIM + t)

        to_near, to_far, to_far_s = pick(RIM + OWN - NEAR, RIM), pick(RIM + OWN - RIM, RIM + NEAR), pick(RIM + OWN - RIM_S, RIM + NEAR)
        for j in range(NI):
            hs[j, :NEAR], hs[j, NEAR:] = even[j, pl.ds(to_near, NEAR)], src[j, pl.ds(to_near, NEAR)]
        for j in range(LOW):
            hs[NI + j, :FAR] = even[j, pl.ds(to_far, FAR)]
            hs[NI + LOW + j, :FAR_S] = src[j, pl.ds(to_far_s, FAR_S)]
        rim_flip.start()
        ends = (RIM - REACH, RIM + OWN + REACH - 8)
        sweep(even, odd, RIM + 6, RIM + 6, high)

        @pl.when(has_outer)
        def _():
            all_of(rn, r_near)

        for which, dst in ((0, even), (1, src)):
            transform(near(rn, which), NEAR, dst, at_outer[0])
        start = pick(*ends)
        sweep(even, odd, start, start, high)
        rim_flip.wait_recv()
        for j in range(NI):
            even[j, pl.ds(at_flip[0], NEAR)], src[j, pl.ds(at_flip[0], NEAR)] = hr[j, :NEAR], hr[j, NEAR:]
        for j in range(LOW):
            even[j, pl.ds(at_flip[1], FAR)] = hr[NI + j, :FAR]
            src[j, pl.ds(at_flip[2], FAR_S)] = hr[NI + LOW + j, :FAR_S]

        start = pick(*ends[::-1])
        sweep(even, odd, start, start, high)

        @pl.when(has_outer)
        def _():
            all_of(rf, r_far)

        transform(far(rf, 0), FAR, even, at_outer[1], forward_low)
        transform(far(rf, 1), FAR_S, src, at_outer[2], forward_low)
        for s in range(SWEEPS):
            relax(low, SWEEPS, s)
            if s < OWN // 8:
                sweep(odd, fin, RIM + 8 * s, 8 * s, high)
        for t in range(0, OWN, 8):
            rows = pl.ds(t, 8)
            x = backward([fin[j, rows] for j in range(NI)])
            for n in range(NI):
                back[n // PER, n % PER, rows] = x[n]
        home = [remote(back.at[i], out.at[:, mine], s_out, r_out, cell, i) for i in range(GROUP)]
        for i in (0, 2, 6, 4, 1, 3, 7, 5):

            @pl.when(inst != i)
            def _():
                home[i].start()

        out[:, mine] = back[inst]
        all_of(back.at[pl.ds(1, GROUP - 1)], s_out)

        all_of(sx.at[pl.ds(1, COMP - 1)], s_own)
        stat_flip.wait_send()
        rim_flip.wait_send()
        all_of(out.at[:, pl.ds(1, COMP - 1)], r_out)

    @pl.when(idle)
    def _():
        pltpu.make_async_copy(sx, sx, s_own).wait()
        pltpu.make_async_copy(out, out, r_out).wait()

    @pl.when(give)
    def _():
        stat_outer.wait_send()

    @pl.when(has_outer)
    def _():
        pltpu.make_async_copy(sn, sn, s_near).wait()
        pltpu.make_async_copy(sf, sf, s_far).wait()


def per_device(initial, source, neighbors, face_weights, damping):
    vmem = pl.BlockSpec(memory_space=pltpu.VMEM)
    f32, i32 = jnp.float32, jnp.int32
    dma = pltpu.SemaphoreType.DMA
    arguments = (initial, source, neighbors, face_weights, damping.reshape(OWN, LANES))
    result = pl.pallas_call(
        kernel,
        out_shape=pltpu.VMEM((PER, COMP, OWN, LANES), f32),
        in_specs=[pl.BlockSpec(memory_space=pltpu.HBM)] * 5,
        out_specs=vmem,
        scratch_shapes=[
            pltpu.VMEM((PER * COMP, OWN * LANES), f32),
            pltpu.VMEM((PER * COMP, OWN * LANES), f32),
            pltpu.VMEM((NEIGH, OWN * LANES), i32),
            pltpu.VMEM((NEIGH, OWN * LANES), f32),
            pltpu.VMEM((OWN, LANES), f32),
            pltpu.VMEM((COMP, 2, PER, OWN, LANES), f32),
            pltpu.VMEM((COMP, M_NEAR, LANES), f32),
            pltpu.VMEM((COMP, M_FAR, LANES), f32),
            pltpu.VMEM((2 * NEIGH + 1, RIM_S, LANES), f32),
            pltpu.VMEM((2 * NEIGH + 1, RIM_S, LANES), f32),
            pltpu.VMEM((GROUP, 2, PER, OWN, LANES), f32),
            pltpu.VMEM((GROUP, M_NEAR, LANES), f32),
            pltpu.VMEM((GROUP, M_FAR, LANES), f32),
            pltpu.VMEM((2 * NEIGH + 1, RIM_S, LANES), f32),
            pltpu.VMEM((2 * NEIGH + 1, RIM_S, LANES), f32),
            pltpu.VMEM((NI + 2 * LOW, 8, LANES), f32),
            pltpu.VMEM((NI + 2 * LOW, 8, LANES), f32),
            pltpu.VMEM((NEIGH, ROWS, LANES), i32),
            pltpu.VMEM((NEIGH, ROWS, LANES), i32),
            pltpu.VMEM((NEIGH, ROWS, LANES), f32),
            pltpu.VMEM((ROWS, LANES), f32),
            pltpu.VMEM((NI, ROWS, LANES), f32),
            pltpu.VMEM((NI, ROWS, LANES), f32),
            pltpu.VMEM((NI, ROWS, LANES), f32),
            pltpu.VMEM((NI, OWN, LANES), f32),
            pltpu.VMEM((GROUP, PER, OWN, LANES), f32),
            dma((5,)), dma, dma, dma, dma((2,)), dma, dma, dma, dma, dma((2,)), dma, dma, dma,
        ],
        compiler_params=pltpu.CompilerParams(
            collective_id=0, has_side_effects=True, vmem_limit_bytes=32 * 1024 * 1024
        ),
    )(*(pltpu.with_memory_space_constraint(x, pltpu.HBM) for x in arguments))
    return result.reshape(PER * COMP, OWN * LANES)


def solution(mesh):
    return jax.shard_map(
        per_device,
        mesh=mesh,
        in_specs=(
            P("inst", "cell"),
            P("inst", "cell"),
            P(None, "cell"),
            P(None, "cell"),
            P("cell"),
        ),
        out_specs=P("inst", "cell"),
        check_vma=False,
    )
```

```python
import math

import jax
import jax.numpy as jnp
from jax import lax
from jax.experimental import pallas as pl
from jax.experimental.pallas import tpu as pltpu
from jax.sharding import PartitionSpec as P

NI = 16
COMP = 5
NEIGH = 4
FREQ = 0.15
RELAX = 0.6
LANES = 128
OWN = 16
SWEEPS_FINE = 2
SWEEPS = 5
REACH = 2
RIM = SWEEPS * REACH
RIM_S = RIM - REACH
ROWS = OWN + 2 * RIM
GROUP = 8
PER = NI // GROUP
NEAR = SWEEPS_FINE * REACH
FAR, FAR_S = RIM - NEAR, RIM_S - NEAR
LOW = 3
M_NEAR, M_FAR = 16, PER * (FAR + FAR_S)
OWNERS = ((1, 2, 3, 4, 6), (0, 1, 2, 4, 6))
MESH = pl.DeviceIdType.MESH
ROOT = math.sqrt(0.5)


def forward(x):
    out = [None] * NI
    p = [x[n] + x[n + 8] for n in range(8)]
    q = [x[n] - x[n + 8] for n in range(8)]
    q0, q4 = q[0] * 0.125, q[4] * 0.125
    d = [None] + [q[n] - q[8 - n] for n in (1, 2, 3)]
    s = [None] + [q[n] + q[8 - n] for n in (1, 2, 3)]
    for k in (1, 3, 5, 7):
        a, b = q0, (q4 if k in (1, 5) else -q4)
        for n in (1, 2, 3):
            a = a + d[n] * (math.cos(math.pi * k * n / 8) / 8)
            b = b + s[n] * (math.sin(math.pi * k * n / 8) / 8)
        out[2 * k - 1], out[2 * k] = a, b
    pp = [p[n] + p[n + 4] for n in range(4)]
    pq = [p[n] - p[n + 4] for n in range(4)]
    a, b = pq[0] * 0.125, pq[2] * 0.125
    d1, s1 = (pq[1] - pq[3]) * (ROOT / 8), (pq[1] + pq[3]) * (ROOT / 8)
    out[3], out[4] = a + d1, s1 + b
    out[11], out[12] = a - d1, s1 - b
    out[7], out[8] = (pp[0] - pp[2]) * 0.125, (pp[1] - pp[3]) * 0.125
    even, odd = (pp[0] + pp[2]) * 0.0625, (pp[1] + pp[3]) * 0.0625
    out[0], out[15] = even + odd, even - odd
    return out


def forward_low(x):
    p = [x[n] + x[n + 8] for n in range(8)]
    q = [x[n] - x[n + 8] for n in range(8)]
    a, b = q[0] * 0.125, q[4] * 0.125
    for n in (1, 2, 3):
        a = a + (q[n] - q[8 - n]) * (math.cos(math.pi * n / 8) / 8)
        b = b + (q[n] + q[8 - n]) * (math.sin(math.pi * n / 8) / 8)
    return [(((p[0] + p[4]) + (p[2] + p[6])) + ((p[1] + p[5]) + (p[3] + p[7]))) * 0.0625, a, b]


def backward(h):
    a = {k: h[2 * k - 1] for k in range(1, 9)}
    a[0] = h[0]
    b = {k: h[2 * k] for k in range(1, 8)}
    odd = [None] * 8
    odd[0] = (a[1] + a[3]) + (a[5] + a[7])
    odd[4] = (b[1] - b[3]) + (b[5] - b[7])
    for n in (1, 2, 3):
        c = s = 0.0
        for k in (1, 3, 5, 7):
            c = c + a[k] * math.cos(math.pi * k * n / 8)
            s = s + b[k] * math.sin(math.pi * k * n / 8)
        odd[n], odd[8 - n] = s + c, s - c
    d, s = (a[2] - a[6]) * ROOT, (b[2] + b[6]) * ROOT
    half = [a[2] + a[6], s + d, b[2] - b[6], s - d]
    up, down = a[0] + a[8], a[0] - a[8]
    quarter = [up + a[4], down + b[4], up - a[4], down - b[4]]
    even = [quarter[n] + half[n] for n in range(4)] + [quarter[n] - half[n] for n in range(4)]
    return [even[n] + odd[n] for n in range(8)] + [even[n] - odd[n] for n in range(8)]


def tiles(start, stop):
    return [min(row, stop - 8) for row in range(start, stop, 8)]


def kernel(
    initial_in, source_in, neighbors_in, weights_in, damping_in, out,
    initial, source, neighbors, weights, damping,
    sx, sn, sf, st_outer, st_flip, ro, rn, rf, got_outer, got_flip, hs, hr,
    lane, step, gain, scale, even, odd, src, fin, back,
    s_in, s_own, s_near, s_far, s_stat, s_rim, r_own, r_near, r_far, r_stat, r_rim, s_out, r_out,
):
    cell, inst = lax.axis_index("cell"), lax.axis_index("inst")
    count = lax.axis_size("cell")
    odd_block = lax.rem(cell, 2)
    is_even = odd_block == 0
    flip = cell + 1 - 2 * odd_block
    beyond = cell - 1 + 2 * odd_block
    has_outer = jnp.logical_and(beyond >= 0, beyond < count)
    outer = jnp.minimum(jnp.maximum(beyond, 0), count - 1)

    def owners(c):
        high = lax.rem(lax.div(c, 2), 2)
        return [OWNERS[0][v] + high * (OWNERS[1][v] - OWNERS[0][v]) for v in range(COMP)]

    here, there = owners(cell), owners(cell + 2)
    mine, owns, serves = 0, 0, 0
    for v in range(COMP):
        hit = (inst == here[v]).astype(jnp.int32)
        mine, owns = mine + v * hit, owns + hit
        serves = serves + (inst == there[v]).astype(jnp.int32)
    busy = owns == 1
    idle = jnp.logical_not(busy)
    give = jnp.logical_and(has_outer, serves == 1)

    barrier = pltpu.get_barrier_semaphore()

    def greet(c, i):
        pl.semaphore_signal(barrier, inc=1, device_id={"cell": c, "inst": i}, device_id_type=MESH)

    @pl.when(busy)
    def _():
        for j in range(1, GROUP):
            greet(cell, lax.rem(inst + j, GROUP))

    load = [
        pltpu.make_async_copy(a, b, s_in.at[j])
        for j, (a, b) in enumerate(
            (
                (initial_in, initial),
                (source_in, source),
                (neighbors_in, neighbors),
                (weights_in, weights),
                (damping_in, damping),
            )
        )
    ]
    for copy in load:
        copy.start()

    @pl.when(busy)
    def _():
        @pl.when(has_outer)
        def _():
            for i in range(GROUP):
                greet(outer, i)

        greet(flip, inst)

    for which, ref in enumerate((initial, source)):
        load[which].wait()
        for n in range(PER):
            for v in range(COMP):
                x = ref[pl.ds(n * COMP + v, 1), :].reshape(OWN, LANES)
                sx[v, which, n] = x
                near_rows = pl.ds((which * PER + n) * NEAR, NEAR)
                sn[v, near_rows] = jnp.where(is_even, x[:NEAR], x[OWN - NEAR :])
                size = (FAR, FAR_S)[which]
                far_rows = pl.ds((n * FAR, PER * FAR + n * FAR_S)[which], size)
                sf[v, far_rows] = jnp.where(is_even, x[NEAR : NEAR + size], x[OWN - NEAR - size : OWN - NEAR])

    pl.semaphore_wait(barrier, COMP * (1 + has_outer.astype(jnp.int32)))

    def remote(a, b, s, r, c, i):
        return pltpu.make_async_remote_copy(
            src_ref=a, dst_ref=b, send_sem=s, recv_sem=r, device_id={"cell": c, "inst": i}, device_id_type=MESH
        )

    own_copy = [remote(sx.at[v], ro.at[inst], s_own, r_own, cell, here[v]) for v in range(COMP)]
    near_copy = [remote(sn.at[v], rn.at[inst], s_near, r_near, outer, there[v]) for v in range(COMP)]
    far_copy = [remote(sf.at[v], rf.at[inst], s_far, r_far, outer, there[v]) for v in range(COMP)]
    stat_outer = remote(st_outer, got_outer, s_stat.at[0], r_stat.at[0], outer, inst)
    stat_flip = remote(st_flip, got_flip, s_stat.at[1], r_stat.at[1], flip, inst)
    rim_flip = remote(hs, hr, s_rim, r_rim, flip, inst)

    for v in range(COMP):

        @pl.when(mine + COMP * (1 - owns) != v)
        def _():
            own_copy[v].start()

    @pl.when(has_outer)
    def _():
        for v in range(COMP):
            near_copy[v].start()

    for copy in load[2:]:
        copy.wait()
    w = [weights[pl.ds(k, 1), :].reshape(OWN, LANES) for k in range(NEIGH)]
    off = [neighbors[pl.ds(k, 1), :].reshape(OWN, LANES) for k in range(NEIGH)]
    m = RELAX / (damping[...] + ((w[0] + w[1]) + (w[2] + w[3])))
    own = pl.ds(RIM, OWN)
    scale[own] = m

    def edges(k, x):
        head, tail = x[:RIM_S], x[OWN - RIM_S :]
        st_outer[k], st_flip[k] = jnp.where(is_even, head, tail), jnp.where(is_even, tail, head)

    edges(2 * NEIGH, m)
    for k in range(NEIGH):
        g = w[k] * m
        position = lax.broadcasted_iota(jnp.int32, (OWN, LANES), 1) + off[k]
        lane[k, own] = position & (LANES - 1)
        step[k, own] = position >> 7
        gain[k, own] = g
        edges(k, off[k].astype(jnp.float32))
        edges(NEIGH + k, g)

    @pl.when(give)
    def _():
        stat_outer.start()

    @pl.when(has_outer)
    def _():
        for v in range(COMP):
            far_copy[v].start()

    hs[NI:] = jnp.zeros((2 * LOW, 8, LANES), jnp.float32)

    @pl.when(busy)
    def _():
        stat_flip.start()
        ro[inst] = sx[mine]

        @pl.when(has_outer)
        def _():
            stat_outer.wait_recv()

        @pl.when(jnp.logical_not(has_outer))
        def _():
            rn[...] = jnp.zeros_like(rn)
            rf[...] = jnp.zeros_like(rf)
            got_outer[...] = jnp.zeros_like(got_outer)

        stat_flip.wait_recv()

        def pick(even_row, odd_row):
            return even_row + odd_block * (odd_row - even_row)

        left, right = (RIM - NEAR, 0, FAR - FAR_S), (RIM + OWN, RIM + OWN + NEAR, RIM + OWN + NEAR)
        at_outer = [pick(a, b) for a, b in zip(left, right)]
        at_flip = [pick(b, a) for a, b in zip(left, right)]
        for start, got in (
            (pick(RIM - RIM_S, RIM + OWN), got_outer),
            (pick(RIM + OWN, RIM - RIM_S), got_flip),
        ):
            rows = pl.ds(start, RIM_S)
            for k in range(NEIGH):
                position = lax.broadcasted_iota(jnp.int32, (RIM_S, LANES), 1) + got[k].astype(jnp.int32)
                lane[k, rows] = position & (LANES - 1)
                step[k, rows] = position >> 7
                gain[k, rows] = got[NEIGH + k]
            scale[rows] = got[2 * NEIGH]

        def transform(read, rows, dst, to, change=forward):
            h = change([read(n) for n in range(NI)])
            for j in range(len(h)):
                dst[j, pl.ds(to, rows)] = h[j]

        def near(ref, which):
            return lambda n: ref[n // PER, pl.ds((which * PER + n % PER) * NEAR, NEAR)]

        def far(ref, which):
            base, size = (0, PER * FAR)[which], (FAR, FAR_S)[which]
            return lambda n: ref[n // PER, pl.ds(base + (n % PER) * size, size)]

        def all_of(ref, sem):
            pltpu.make_async_copy(ref, ref, sem).wait()

        def sweep(old, new, start, to, harmonics):
            rows = pl.ds(start, 8)
            m = scale[rows]
            names = [j for k in harmonics for j in ((2 * k - 1, 2 * k) if 0 < k < 8 else (max(2 * k - 1, 0),))]
            total = {}
            for k in harmonics:
                if k in (0, 8):
                    j = max(2 * k - 1, 0)
                    total[j] = (1.0 - RELAX) * old[j, rows] + m * src[j, rows]
                else:
                    a, b = 2 * k - 1, 2 * k
                    xa, xb = old[a, rows], old[b, rows]
                    total[a] = (1.0 - RELAX) * xa + m * (src[a, rows] - (FREQ * k) * xb)
                    total[b] = (1.0 - RELAX) * xb + m * (src[b, rows] + (FREQ * k) * xa)
            for k in range(NEIGH):
                sign = 1 if k % 2 else -1
                index, by, g = lane[k, rows], step[k, rows], gain[k, rows]
                near, next_ = by == 0, by == sign
                for j in names:
                    pick = [
                        jnp.take_along_axis(old[j, pl.ds(start + sign * d, 8)], index, axis=1, mode="promise_in_bounds")
                        for d in range(REACH + 1)
                    ]
                    total[j] = total[j] + g * jnp.where(near, pick[0], jnp.where(next_, pick[1], pick[2]))
            for j in names:
                new[j, pl.ds(to, 8)] = total[j]

        low, high = (0, 1), tuple(range(2, 9))
        buffers = (even, odd)
        def relax(harmonics, sweeps, s):
            wide = (sweeps - 1 - s) * REACH
            old, new = buffers[s % 2], buffers[(s + 1) % 2]
            for start in tiles(RIM - wide, RIM + OWN + wide):
                if s < sweeps - 1:
                    sweep(old, new, start, start, harmonics)
                else:
                    sweep(old, fin, start, start - RIM, harmonics)

        all_of(ro.at[pl.ds(1, GROUP - 1)], r_own)
        for t in range(0, OWN, 8):
            for which, dst in ((0, even), (1, src)):
                transform(lambda n: ro[n // PER, which, n % PER, pl.ds(t, 8)], 8, dst, RIM + t)

        to_near, to_far, to_far_s = pick(RIM + OWN - NEAR, RIM), pick(RIM + OWN - RIM, RIM + NEAR), pick(RIM + OWN - RIM_S, RIM + NEAR)
        for j in range(NI):
            hs[j, :NEAR], hs[j, NEAR:] = even[j, pl.ds(to_near, NEAR)], src[j, pl.ds(to_near, NEAR)]
        for j in range(LOW):
            hs[NI + j, :FAR] = even[j, pl.ds(to_far, FAR)]
            hs[NI + LOW + j, :FAR_S] = src[j, pl.ds(to_far_s, FAR_S)]
        rim_flip.start()
        ends = (RIM - REACH, RIM + OWN + REACH - 8)
        sweep(even, odd, RIM + 6, RIM + 6, high)

        @pl.when(has_outer)
        def _():
            all_of(rn, r_near)

        for which, dst in ((0, even), (1, src)):
            transform(near(rn, which), NEAR, dst, at_outer[0])
        start = pick(*ends)
        sweep(even, odd, start, start, high)
        rim_flip.wait_recv()
        for j in range(NI):
            even[j, pl.ds(at_flip[0], NEAR)], src[j, pl.ds(at_flip[0], NEAR)] = hr[j, :NEAR], hr[j, NEAR:]
        for j in range(LOW):
            even[j, pl.ds(at_flip[1], FAR)] = hr[NI + j, :FAR]
            src[j, pl.ds(at_flip[2], FAR_S)] = hr[NI + LOW + j, :FAR_S]

        start = pick(*ends[::-1])
        sweep(even, odd, start, start, high)

        @pl.when(has_outer)
        def _():
            all_of(rf, r_far)

        transform(far(rf, 0), FAR, even, at_outer[1], forward_low)
        transform(far(rf, 1), FAR_S, src, at_outer[2], forward_low)
        for s in range(SWEEPS):
            relax(low, SWEEPS, s)
            if s < OWN // 8:
                sweep(odd, fin, RIM + 8 * s, 8 * s, high)
        for t in range(0, OWN, 8):
            rows = pl.ds(t, 8)
            x = backward([fin[j, rows] for j in range(NI)])
            for n in range(NI):
                back[n // PER, n % PER, rows] = x[n]
        home = [remote(back.at[i], out.at[:, mine], s_out, r_out, cell, i) for i in range(GROUP)]
        for i in (0, 2, 6, 4, 1, 3, 7, 5):

            @pl.when(inst != i)
            def _():
                home[i].start()

        out[:, mine] = back[inst]
        all_of(back.at[pl.ds(1, GROUP - 1)], s_out)

        all_of(sx.at[pl.ds(1, COMP - 1)], s_own)
        stat_flip.wait_send()
        rim_flip.wait_send()
        all_of(out.at[:, pl.ds(1, COMP - 1)], r_out)

    @pl.when(idle)
    def _():
        pltpu.make_async_copy(sx, sx, s_own).wait()
        pltpu.make_async_copy(out, out, r_out).wait()

    @pl.when(give)
    def _():
        stat_outer.wait_send()

    @pl.when(has_outer)
    def _():
        pltpu.make_async_copy(sn, sn, s_near).wait()
        pltpu.make_async_copy(sf, sf, s_far).wait()


def per_device(initial, source, neighbors, face_weights, damping):
    vmem = pl.BlockSpec(memory_space=pltpu.VMEM)
    f32, i32 = jnp.float32, jnp.int32
    dma = pltpu.SemaphoreType.DMA
    arguments = (initial, source, neighbors, face_weights, damping.reshape(OWN, LANES))
    result = pl.pallas_call(
        kernel,
        out_shape=pltpu.VMEM((PER, COMP, OWN, LANES), f32),
        in_specs=[pl.BlockSpec(memory_space=pltpu.HBM)] * 5,
        out_specs=vmem,
        scratch_shapes=[
            pltpu.VMEM((PER * COMP, OWN * LANES), f32),
            pltpu.VMEM((PER * COMP, OWN * LANES), f32),
            pltpu.VMEM((NEIGH, OWN * LANES), i32),
            pltpu.VMEM((NEIGH, OWN * LANES), f32),
            pltpu.VMEM((OWN, LANES), f32),
            pltpu.VMEM((COMP, 2, PER, OWN, LANES), f32),
            pltpu.VMEM((COMP, M_NEAR, LANES), f32),
            pltpu.VMEM((COMP, M_FAR, LANES), f32),
            pltpu.VMEM((2 * NEIGH + 1, RIM_S, LANES), f32),
            pltpu.VMEM((2 * NEIGH + 1, RIM_S, LANES), f32),
            pltpu.VMEM((GROUP, 2, PER, OWN, LANES), f32),
            pltpu.VMEM((GROUP, M_NEAR, LANES), f32),
            pltpu.VMEM((GROUP, M_FAR, LANES), f32),
            pltpu.VMEM((2 * NEIGH + 1, RIM_S, LANES), f32),
            pltpu.VMEM((2 * NEIGH + 1, RIM_S, LANES), f32),
            pltpu.VMEM((NI + 2 * LOW, 8, LANES), f32),
            pltpu.VMEM((NI + 2 * LOW, 8, LANES), f32),
            pltpu.VMEM((NEIGH, ROWS, LANES), i32),
            pltpu.VMEM((NEIGH, ROWS, LANES), i32),
            pltpu.VMEM((NEIGH, ROWS, LANES), f32),
            pltpu.VMEM((ROWS, LANES), f32),
            pltpu.VMEM((NI, ROWS, LANES), f32),
            pltpu.VMEM((NI, ROWS, LANES), f32),
            pltpu.VMEM((NI, ROWS, LANES), f32),
            pltpu.VMEM((NI, OWN, LANES), f32),
            pltpu.VMEM((GROUP, PER, OWN, LANES), f32),
            dma((5,)), dma, dma, dma, dma((2,)), dma, dma, dma, dma, dma((2,)), dma, dma, dma,
        ],
        compiler_params=pltpu.CompilerParams(
            collective_id=0, has_side_effects=True, vmem_limit_bytes=32 * 1024 * 1024
        ),
    )(*(pltpu.with_memory_space_constraint(x, pltpu.HBM) for x in arguments))
    return result.reshape(PER * COMP, OWN * LANES)


def solution(mesh):
    return jax.shard_map(
        per_device,
        mesh=mesh,
        in_specs=(
            P("inst", "cell"),
            P("inst", "cell"),
            P(None, "cell"),
            P(None, "cell"),
            P("cell"),
        ),
        out_specs=P("inst", "cell"),
        check_vma=False,
    )
```

```python
import math

import jax
import jax.numpy as jnp
from jax import lax
from jax.experimental import pallas as pl
from jax.experimental.pallas import tpu as pltpu
from jax.sharding import PartitionSpec as P

NI = 16
COMP = 5
NEIGH = 4
FREQ = 0.15
RELAX = 0.6
LANES = 128
OWN = 16
SWEEPS_FINE = 2
SWEEPS = 5
REACH = 2
RIM = SWEEPS * REACH
RIM_S = RIM - REACH
ROWS = OWN + 2 * RIM
GROUP = 8
PER = NI // GROUP
NEAR = SWEEPS_FINE * REACH
FAR, FAR_S = RIM - NEAR, RIM_S - NEAR
LOW = 3
M_NEAR, M_FAR = 16, PER * (FAR + FAR_S)
OWNERS = ((1, 2, 3, 4, 6), (0, 1, 2, 4, 6))
MESH = pl.DeviceIdType.MESH
ROOT = math.sqrt(0.5)


def forward(x):
    out = [None] * NI
    p = [x[n] + x[n + 8] for n in range(8)]
    q = [x[n] - x[n + 8] for n in range(8)]
    q0, q4 = q[0] * 0.125, q[4] * 0.125
    d = [None] + [q[n] - q[8 - n] for n in (1, 2, 3)]
    s = [None] + [q[n] + q[8 - n] for n in (1, 2, 3)]
    for k in (1, 3, 5, 7):
        a, b = q0, (q4 if k in (1, 5) else -q4)
        for n in (1, 2, 3):
            a = a + d[n] * (math.cos(math.pi * k * n / 8) / 8)
            b = b + s[n] * (math.sin(math.pi * k * n / 8) / 8)
        out[2 * k - 1], out[2 * k] = a, b
    pp = [p[n] + p[n + 4] for n in range(4)]
    pq = [p[n] - p[n + 4] for n in range(4)]
    a, b = pq[0] * 0.125, pq[2] * 0.125
    d1, s1 = (pq[1] - pq[3]) * (ROOT / 8), (pq[1] + pq[3]) * (ROOT / 8)
    out[3], out[4] = a + d1, s1 + b
    out[11], out[12] = a - d1, s1 - b
    out[7], out[8] = (pp[0] - pp[2]) * 0.125, (pp[1] - pp[3]) * 0.125
    even, odd = (pp[0] + pp[2]) * 0.0625, (pp[1] + pp[3]) * 0.0625
    out[0], out[15] = even + odd, even - odd
    return out


def forward_low(x):
    p = [x[n] + x[n + 8] for n in range(8)]
    q = [x[n] - x[n + 8] for n in range(8)]
    a, b = q[0] * 0.125, q[4] * 0.125
    for n in (1, 2, 3):
        a = a + (q[n] - q[8 - n]) * (math.cos(math.pi * n / 8) / 8)
        b = b + (q[n] + q[8 - n]) * (math.sin(math.pi * n / 8) / 8)
    return [(((p[0] + p[4]) + (p[2] + p[6])) + ((p[1] + p[5]) + (p[3] + p[7]))) * 0.0625, a, b]


def backward(h):
    a = {k: h[2 * k - 1] for k in range(1, 9)}
    a[0] = h[0]
    b = {k: h[2 * k] for k in range(1, 8)}
    odd = [None] * 8
    odd[0] = (a[1] + a[3]) + (a[5] + a[7])
    odd[4] = (b[1] - b[3]) + (b[5] - b[7])
    for n in (1, 2, 3):
        c = s = 0.0
        for k in (1, 3, 5, 7):
            c = c + a[k] * math.cos(math.pi * k * n / 8)
            s = s + b[k] * math.sin(math.pi * k * n / 8)
        odd[n], odd[8 - n] = s + c, s - c
    d, s = (a[2] - a[6]) * ROOT, (b[2] + b[6]) * ROOT
    half = [a[2] + a[6], s + d, b[2] - b[6], s - d]
    up, down = a[0] + a[8], a[0] - a[8]
    quarter = [up + a[4], down + b[4], up - a[4], down - b[4]]
    even = [quarter[n] + half[n] for n in range(4)] + [quarter[n] - half[n] for n in range(4)]
    return [even[n] + odd[n] for n in range(8)] + [even[n] - odd[n] for n in range(8)]


def tiles(start, stop):
    return [min(row, stop - 8) for row in range(start, stop, 8)]


def kernel(
    initial_in, source_in, neighbors_in, weights_in, damping_in, out,
    initial, source, neighbors, weights, damping,
    sx, sn, sf, st_outer, st_flip, ro, rn, rf, got_outer, got_flip, hs, hr,
    lane, step, gain, scale, even, odd, src, fin, back,
    s_in, s_own, s_near, s_far, s_stat, s_rim, r_own, r_near, r_far, r_stat, r_rim, s_out, r_out,
):
    cell, inst = lax.axis_index("cell"), lax.axis_index("inst")
    count = lax.axis_size("cell")
    odd_block = lax.rem(cell, 2)
    is_even = odd_block == 0
    flip = cell + 1 - 2 * odd_block
    beyond = cell - 1 + 2 * odd_block
    has_outer = jnp.logical_and(beyond >= 0, beyond < count)
    outer = jnp.minimum(jnp.maximum(beyond, 0), count - 1)

    def owners(c):
        high = lax.rem(lax.div(c, 2), 2)
        return [OWNERS[0][v] + high * (OWNERS[1][v] - OWNERS[0][v]) for v in range(COMP)]

    here, there = owners(cell), owners(cell + 2)
    mine, owns, serves = 0, 0, 0
    for v in range(COMP):
        hit = (inst == here[v]).astype(jnp.int32)
        mine, owns = mine + v * hit, owns + hit
        serves = serves + (inst == there[v]).astype(jnp.int32)
    busy = owns == 1
    idle = jnp.logical_not(busy)
    give = jnp.logical_and(has_outer, serves == 1)

    barrier = pltpu.get_barrier_semaphore()

    def greet(c, i):
        pl.semaphore_signal(barrier, inc=1, device_id={"cell": c, "inst": i}, device_id_type=MESH)

    @pl.when(busy)
    def _():
        for j in range(1, GROUP):
            greet(cell, lax.rem(inst + j, GROUP))

    load = [
        pltpu.make_async_copy(a, b, s_in.at[j])
        for j, (a, b) in enumerate(
            (
                (initial_in, initial),
                (source_in, source),
                (neighbors_in, neighbors),
                (weights_in, weights),
                (damping_in, damping),
            )
        )
    ]
    for copy in load:
        copy.start()

    @pl.when(busy)
    def _():
        @pl.when(has_outer)
        def _():
            for i in range(GROUP):
                greet(outer, i)

        greet(flip, inst)

    for copy in load[2:]:
        copy.wait()
    w = [weights[pl.ds(k, 1), :].reshape(OWN, LANES) for k in range(NEIGH)]
    off = [neighbors[pl.ds(k, 1), :].reshape(OWN, LANES) for k in range(NEIGH)]
    m = RELAX / (damping[...] + ((w[0] + w[1]) + (w[2] + w[3])))
    own = pl.ds(RIM, OWN)
    scale[own] = m

    def edges(k, x):
        head, tail = x[:RIM_S], x[OWN - RIM_S :]
        st_outer[k], st_flip[k] = jnp.where(is_even, head, tail), jnp.where(is_even, tail, head)

    edges(2 * NEIGH, m)
    for k in range(NEIGH):
        g = w[k] * m
        position = lax.broadcasted_iota(jnp.int32, (OWN, LANES), 1) + off[k]
        lane[k, own] = position & (LANES - 1)
        step[k, own] = position >> 7
        gain[k, own] = g
        edges(k, off[k].astype(jnp.float32))
        edges(NEIGH + k, g)

    hs[NI:] = jnp.zeros((2 * LOW, 8, LANES), jnp.float32)

    for which, ref in enumerate((initial, source)):
        load[which].wait()
        for n in range(PER):
            for v in range(COMP):
                x = ref[pl.ds(n * COMP + v, 1), :].reshape(OWN, LANES)
                sx[v, which, n] = x
                near_rows = pl.ds((which * PER + n) * NEAR, NEAR)
                sn[v, near_rows] = jnp.where(is_even, x[:NEAR], x[OWN - NEAR :])
                size = (FAR, FAR_S)[which]
                far_rows = pl.ds((n * FAR, PER * FAR + n * FAR_S)[which], size)
                sf[v, far_rows] = jnp.where(is_even, x[NEAR : NEAR + size], x[OWN - NEAR - size : OWN - NEAR])

    pl.semaphore_wait(barrier, COMP * (1 + has_outer.astype(jnp.int32)))

    def remote(a, b, s, r, c, i):
        return pltpu.make_async_remote_copy(
            src_ref=a, dst_ref=b, send_sem=s, recv_sem=r, device_id={"cell": c, "inst": i}, device_id_type=MESH
        )

    own_copy = [remote(sx.at[v], ro.at[inst], s_own, r_own, cell, here[v]) for v in range(COMP)]
    near_copy = [remote(sn.at[v], rn.at[inst], s_near, r_near, outer, there[v]) for v in range(COMP)]
    far_copy = [remote(sf.at[v], rf.at[inst], s_far, r_far, outer, there[v]) for v in range(COMP)]
    stat_outer = remote(st_outer, got_outer, s_stat.at[0], r_stat.at[0], outer, inst)
    stat_flip = remote(st_flip, got_flip, s_stat.at[1], r_stat.at[1], flip, inst)
    rim_flip = remote(hs, hr, s_rim, r_rim, flip, inst)

    for v in range(COMP):

        @pl.when(mine + COMP * (1 - owns) != v)
        def _():
            own_copy[v].start()

    @pl.when(has_outer)
    def _():
        for v in range(COMP):
            near_copy[v].start()

    @pl.when(give)
    def _():
        stat_outer.start()

    @pl.when(has_outer)
    def _():
        for v in range(COMP):
            far_copy[v].start()

    @pl.when(busy)
    def _():
        stat_flip.start()
        ro[inst] = sx[mine]

        @pl.when(has_outer)
        def _():
            stat_outer.wait_recv()

        @pl.when(jnp.logical_not(has_outer))
        def _():
            rn[...] = jnp.zeros_like(rn)
            rf[...] = jnp.zeros_like(rf)
            got_outer[...] = jnp.zeros_like(got_outer)

        stat_flip.wait_recv()

        def pick(even_row, odd_row):
            return even_row + odd_block * (odd_row - even_row)

        left, right = (RIM - NEAR, 0, FAR - FAR_S), (RIM + OWN, RIM + OWN + NEAR, RIM + OWN + NEAR)
        at_outer = [pick(a, b) for a, b in zip(left, right)]
        at_flip = [pick(b, a) for a, b in zip(left, right)]
        for start, got in (
            (pick(RIM - RIM_S, RIM + OWN), got_outer),
            (pick(RIM + OWN, RIM - RIM_S), got_flip),
        ):
            rows = pl.ds(start, RIM_S)
            for k in range(NEIGH):
                position = lax.broadcasted_iota(jnp.int32, (RIM_S, LANES), 1) + got[k].astype(jnp.int32)
                lane[k, rows] = position & (LANES - 1)
                step[k, rows] = position >> 7
                gain[k, rows] = got[NEIGH + k]
            scale[rows] = got[2 * NEIGH]

        def transform(read, rows, dst, to, change=forward):
            h = change([read(n) for n in range(NI)])
            for j in range(len(h)):
                dst[j, pl.ds(to, rows)] = h[j]

        def near(ref, which):
            return lambda n: ref[n // PER, pl.ds((which * PER + n % PER) * NEAR, NEAR)]

        def far(ref, which):
            base, size = (0, PER * FAR)[which], (FAR, FAR_S)[which]
            return lambda n: ref[n // PER, pl.ds(base + (n % PER) * size, size)]

        def all_of(ref, sem):
            pltpu.make_async_copy(ref, ref, sem).wait()

        def sweep(old, new, start, to, harmonics):
            rows = pl.ds(start, 8)
            m = scale[rows]
            names = [j for k in harmonics for j in ((2 * k - 1, 2 * k) if 0 < k < 8 else (max(2 * k - 1, 0),))]
            total = {}
            for k in harmonics:
                if k in (0, 8):
                    j = max(2 * k - 1, 0)
                    total[j] = (1.0 - RELAX) * old[j, rows] + m * src[j, rows]
                else:
                    a, b = 2 * k - 1, 2 * k
                    xa, xb = old[a, rows], old[b, rows]
                    total[a] = (1.0 - RELAX) * xa + m * (src[a, rows] - (FREQ * k) * xb)
                    total[b] = (1.0 - RELAX) * xb + m * (src[b, rows] + (FREQ * k) * xa)
            for k in range(NEIGH):
                sign = 1 if k % 2 else -1
                index, by, g = lane[k, rows], step[k, rows], gain[k, rows]
                near, next_ = by == 0, by == sign
                for j in names:
                    pick = [
                        jnp.take_along_axis(old[j, pl.ds(start + sign * d, 8)], index, axis=1, mode="promise_in_bounds")
                        for d in range(REACH + 1)
                    ]
                    total[j] = total[j] + g * jnp.where(near, pick[0], jnp.where(next_, pick[1], pick[2]))
            for j in names:
                new[j, pl.ds(to, 8)] = total[j]

        low, high = (0, 1), tuple(range(2, 9))
        buffers = (even, odd)
        def relax(harmonics, sweeps, s):
            wide = (sweeps - 1 - s) * REACH
            old, new = buffers[s % 2], buffers[(s + 1) % 2]
            for start in tiles(RIM - wide, RIM + OWN + wide):
                if s < sweeps - 1:
                    sweep(old, new, start, start, harmonics)
                else:
                    sweep(old, fin, start, start - RIM, harmonics)

        all_of(ro.at[pl.ds(1, GROUP - 1)], r_own)
        for t in range(0, OWN, 8):
            for which, dst in ((0, even), (1, src)):
                transform(lambda n: ro[n // PER, which, n % PER, pl.ds(t, 8)], 8, dst, RIM + t)

        to_near, to_far, to_far_s = pick(RIM + OWN - NEAR, RIM), pick(RIM + OWN - RIM, RIM + NEAR), pick(RIM + OWN - RIM_S, RIM + NEAR)
        for j in range(NI):
            hs[j, :NEAR], hs[j, NEAR:] = even[j, pl.ds(to_near, NEAR)], src[j, pl.ds(to_near, NEAR)]
        for j in range(LOW):
            hs[NI + j, :FAR] = even[j, pl.ds(to_far, FAR)]
            hs[NI + LOW + j, :FAR_S] = src[j, pl.ds(to_far_s, FAR_S)]
        rim_flip.start()
        ends = (RIM - REACH, RIM + OWN + REACH - 8)
        sweep(even, odd, RIM + 6, RIM + 6, high)

        @pl.when(has_outer)
        def _():
            all_of(rn, r_near)

        for which, dst in ((0, even), (1, src)):
            transform(near(rn, which), NEAR, dst, at_outer[0])
        start = pick(*ends)
        sweep(even, odd, start, start, high)
        rim_flip.wait_recv()
        for j in range(NI):
            even[j, pl.ds(at_flip[0], NEAR)], src[j, pl.ds(at_flip[0], NEAR)] = hr[j, :NEAR], hr[j, NEAR:]
        for j in range(LOW):
            even[j, pl.ds(at_flip[1], FAR)] = hr[NI + j, :FAR]
            src[j, pl.ds(at_flip[2], FAR_S)] = hr[NI + LOW + j, :FAR_S]

        start = pick(*ends[::-1])
        sweep(even, odd, start, start, high)

        for t in range(0, OWN, 8):
            sweep(even, odd, RIM + t, RIM + t, low)
        sweep(odd, fin, RIM, 0, high)

        @pl.when(has_outer)
        def _():
            all_of(rf, r_far)

        transform(far(rf, 0), FAR, even, at_outer[1], forward_low)
        transform(far(rf, 1), FAR_S, src, at_outer[2], forward_low)
        for start in (RIM - RIM_S, RIM + OWN):
            sweep(even, odd, start, start, low)
        sweep(odd, fin, RIM + 8, 8, high)
        for s in range(1, SWEEPS):
            relax(low, SWEEPS, s)
        for t in range(0, OWN, 8):
            rows = pl.ds(t, 8)
            x = backward([fin[j, rows] for j in range(NI)])
            for n in range(NI):
                back[n // PER, n % PER, rows] = x[n]
        home = [remote(back.at[i], out.at[:, mine], s_out, r_out, cell, i) for i in range(GROUP)]
        for i in (0, 2, 6, 4, 1, 3, 7, 5):

            @pl.when(inst != i)
            def _():
                home[i].start()

        out[:, mine] = back[inst]
        all_of(back.at[pl.ds(1, GROUP - 1)], s_out)

        all_of(sx.at[pl.ds(1, COMP - 1)], s_own)
        stat_flip.wait_send()
        rim_flip.wait_send()
        all_of(out.at[:, pl.ds(1, COMP - 1)], r_out)

    @pl.when(idle)
    def _():
        pltpu.make_async_copy(sx, sx, s_own).wait()
        pltpu.make_async_copy(out, out, r_out).wait()

    @pl.when(give)
    def _():
        stat_outer.wait_send()

    @pl.when(has_outer)
    def _():
        pltpu.make_async_copy(sn, sn, s_near).wait()
        pltpu.make_async_copy(sf, sf, s_far).wait()


def per_device(initial, source, neighbors, face_weights, damping):
    vmem = pl.BlockSpec(memory_space=pltpu.VMEM)
    f32, i32 = jnp.float32, jnp.int32
    dma = pltpu.SemaphoreType.DMA
    arguments = (initial, source, neighbors, face_weights, damping.reshape(OWN, LANES))
    result = pl.pallas_call(
        kernel,
        out_shape=pltpu.VMEM((PER, COMP, OWN, LANES), f32),
        in_specs=[pl.BlockSpec(memory_space=pltpu.HBM)] * 5,
        out_specs=vmem,
        scratch_shapes=[
            pltpu.VMEM((PER * COMP, OWN * LANES), f32),
            pltpu.VMEM((PER * COMP, OWN * LANES), f32),
            pltpu.VMEM((NEIGH, OWN * LANES), i32),
            pltpu.VMEM((NEIGH, OWN * LANES), f32),
            pltpu.VMEM((OWN, LANES), f32),
            pltpu.VMEM((COMP, 2, PER, OWN, LANES), f32),
            pltpu.VMEM((COMP, M_NEAR, LANES), f32),
            pltpu.VMEM((COMP, M_FAR, LANES), f32),
            pltpu.VMEM((2 * NEIGH + 1, RIM_S, LANES), f32),
            pltpu.VMEM((2 * NEIGH + 1, RIM_S, LANES), f32),
            pltpu.VMEM((GROUP, 2, PER, OWN, LANES), f32),
            pltpu.VMEM((GROUP, M_NEAR, LANES), f32),
            pltpu.VMEM((GROUP, M_FAR, LANES), f32),
            pltpu.VMEM((2 * NEIGH + 1, RIM_S, LANES), f32),
            pltpu.VMEM((2 * NEIGH + 1, RIM_S, LANES), f32),
            pltpu.VMEM((NI + 2 * LOW, 8, LANES), f32),
            pltpu.VMEM((NI + 2 * LOW, 8, LANES), f32),
            pltpu.VMEM((NEIGH, ROWS, LANES), i32),
            pltpu.VMEM((NEIGH, ROWS, LANES), i32),
            pltpu.VMEM((NEIGH, ROWS, LANES), f32),
            pltpu.VMEM((ROWS, LANES), f32),
            pltpu.VMEM((NI, ROWS, LANES), f32),
            pltpu.VMEM((NI, ROWS, LANES), f32),
            pltpu.VMEM((NI, ROWS, LANES), f32),
            pltpu.VMEM((NI, OWN, LANES), f32),
            pltpu.VMEM((GROUP, PER, OWN, LANES), f32),
            dma((5,)), dma, dma, dma, dma((2,)), dma, dma, dma, dma, dma((2,)), dma, dma, dma,
        ],
        compiler_params=pltpu.CompilerParams(
            collective_id=0, has_side_effects=True, vmem_limit_bytes=32 * 1024 * 1024
        ),
    )(*(pltpu.with_memory_space_constraint(x, pltpu.HBM) for x in arguments))
    return result.reshape(PER * COMP, OWN * LANES)


def solution(mesh):
    return jax.shard_map(
        per_device,
        mesh=mesh,
        in_specs=(
            P("inst", "cell"),
            P("inst", "cell"),
            P(None, "cell"),
            P(None, "cell"),
            P("cell"),
        ),
        out_specs=P("inst", "cell"),
        check_vma=False,
    )
```
